128 devices in a mesh: store: 4 (over z), req: 32 (over x, y, core).
Axes of the slice: x: 4, y: 4, z: 4, core: 2. Of those that a mesh axis runs over, the one named last changes fastest.
Arguments:
- hidden: bfloat16 [20480, 8192], P('req', 'store'), may hold values from -6 to 6
- norm_gain: float32 [8192], replicated, may hold values from 0.1 to 1.9
- w_query: bfloat16 [8192, 4096], P(None, 'store'), may hold values from -0.0625 to 0.0625
- w_key: bfloat16 [8192, 512], P(None, 'store'), may hold values from -0.0625 to 0.0625
- w_value: bfloat16 [8192, 512], P(None, 'store'), may hold values from -0.0625 to 0.0625
- passage_cache: bfloat16 [256, 4, 256, 256], P('req', 'store'), may hold values from -6 to 6
- sys_cache: bfloat16 [1024, 4, 256], P('req', 'store'), may hold values from -800 to 800
- passage_place: int32 [256], replicated, may hold values from 0 to 255, as said below
- passage_ids: int32 [256, 4], P('req'), may hold values from 0 to 255, as said below
- passage_count: int32 [256], P('req'), may hold values from 3 to 4
- recompute_pos: int32 [256, 80], P('req'), may hold values from 0 to 1023, as said below
Outputs:
- attended: bfloat16 [20480, 4096], P('req', 'store')
The draws below stay inside these ranges and needn't reach their ends.
Inputs may be any that keep to these rules, and one draw needn't show every extreme that they name: `passage_place`: A permutation of the storage positions. `passage_ids`: slot j of request r is valid when j < passage_count[r]; padded slots hold ids too. Over the requests of one index of req, at most 2 valid slots name passages whose storage position lies on one index of req (passage_place // 8); ids may repeat. `recompute_pos`: distinct and rising along each row; entries at or past passage_count * 256 of their request are padding.
All inputs are finite; a program needn't handle non-finite values.
Results may differ from the reference program's by a relative error of at most 0.023.
The reference program's roundings to bfloat16 on the way (of `normed`, `queries`, `context` and `weights_low`) count: a program that leaves them out, or rounds other values in their place, can miss the bound.
Values may be sent and summed in bfloat16 or wider, within the bound.
A program may use at most 192 MiB of HBM per device.

```python
import jax
import jax.numpy as jnp
from jax import lax

D = 8192
HD = 128
GROUP = 8
PT = 256
MAXP = 4
RT = 80
REQ_DEV = 8
PASS_DEV = 8
KVH = 4
HQ = 32
REQS = 256
TOKS = 20480
PASSAGES = 256
SYS = 1024
CAP = 2
N_REQ = 32


def shared_place(key):
    return jax.random.permutation(jax.random.fold_in(key, 101), PASSAGES).astype(jnp.int32)


def shared_counts(key):
    return jax.random.randint(jax.random.fold_in(key, 102), (REQS,), 3, MAXP + 1).astype(jnp.int32)


def draw_passage_place(key, part):
    placed = shared_place(key)
    return placed


def draw_passage_count(key, part):
    counted = shared_counts(key)
    return counted


def draw_passage_ids(key, part):
    placed = shared_place(key)
    inverse = jnp.argsort(placed).astype(jnp.int32)
    key = jax.random.fold_in(key, 7)
    slots = REQ_DEV * MAXP
    first, second, third = jax.random.split(key, 3)
    source_order = jax.vmap(lambda k: jax.random.permutation(k, N_REQ))(jax.random.split(first, N_REQ))
    slot_order = jax.vmap(lambda k: jax.random.permutation(k, slots))(jax.random.split(second, N_REQ))
    sources = jnp.take_along_axis(source_order, slot_order // CAP, axis=1)
    stored_rows = jax.random.randint(third, (N_REQ, slots), 0, PASS_DEV)
    spots = (sources * PASS_DEV + stored_rows).astype(jnp.int32)
    return inverse[spots].reshape(REQS, MAXP).astype(jnp.int32)


def draw_recompute_pos(key, part):
    key = jax.random.fold_in(key, 9)
    length = MAXP * PT
    scores = jax.vmap(lambda k: jax.random.permutation(k, length))(jax.random.split(key, REQS)).astype(jnp.int32)
    offsets = jnp.arange(length, dtype=jnp.int32)
    rows = jnp.arange(REQS, dtype=jnp.int32)
    first_row = rows[:, None] == 0
    scores = jnp.where(first_row & (offsets[None, :] == 0), length, scores)
    scores = jnp.where(first_row & (offsets[None, :] == length - 1), length + 1, scores)
    chosen = lax.top_k(scores, RT)[1]
    return jnp.sort(chosen, axis=1).astype(jnp.int32)


def draw_sys_cache(key, part):
    key = jax.random.fold_in(key, 11)
    first = jax.random.fold_in(key, 0)
    base = jnp.clip(jax.random.normal(first, (SYS, KVH, 2 * HD), jnp.float32), -4.0, 4.0)
    return base.astype(jnp.bfloat16)


def block_scale(own_key, shape, cuts, low, high):
    gain = 1.0
    for dim, blocks in cuts:
        steps = jax.random.uniform(jax.random.fold_in(jax.random.fold_in(own_key, 6), dim), (blocks,), jnp.float32, low / len(cuts), high / len(cuts))
        gain = gain * jnp.repeat(jnp.exp(steps), shape[dim] // blocks).reshape((-1,) + (1,) * (len(shape) - 1 - dim))
    return gain


def normal_values(stream_key, dims, scale, bound, cuts=(), kind=jnp.bfloat16):
    values = scale * jax.random.normal(stream_key, dims, jnp.float32)
    if cuts:
        values = values * block_scale(stream_key, dims, cuts, -0.22, 0.18)
    return jnp.clip(values, -bound, bound).astype(kind)


def setup_inputs(seed: int = 0) -> dict:
    splits = jax.random.split(jax.random.key(seed), 12)
    hidden = normal_values(splits[0], (TOKS, D), 1.0, 6.0, ((0, 32), (1, 4)))
    norm_gain = jnp.clip(1.0 + 0.18 * jax.random.normal(splits[1], (D,), jnp.float32), 0.1, 1.9)
    w_query = normal_values(splits[2], (D, HQ * HD), D ** -0.5, 0.0625, ((1, 4),))
    w_key = normal_values(splits[3], (D, KVH * HD), D ** -0.5, 0.0625, ((1, 4),))
    w_value = normal_values(splits[4], (D, KVH * HD), D ** -0.5, 0.0625, ((1, 4),))
    passage_cache = normal_values(splits[5], (PASSAGES, KVH, PT, 2 * HD), 1.0, 6.0, ((0, 32), (1, 4)))
    sys_cache = draw_sys_cache(jax.random.fold_in(splits[11], 71), 0)
    passage_place = draw_passage_place(jax.random.fold_in(splits[11], 71), 0)
    passage_ids = draw_passage_ids(jax.random.fold_in(splits[11], 71), 0)
    passage_count = draw_passage_count(jax.random.fold_in(splits[11], 71), 0)
    recompute_pos = draw_recompute_pos(jax.random.fold_in(splits[11], 71), 0)
    return dict(hidden=hidden, norm_gain=norm_gain, w_query=w_query, w_key=w_key, w_value=w_value, passage_cache=passage_cache, sys_cache=sys_cache, passage_place=passage_place, passage_ids=passage_ids, passage_count=passage_count, recompute_pos=recompute_pos)


def reference(hidden, norm_gain, w_query, w_key, w_value, passage_cache, sys_cache, passage_place, passage_ids, passage_count, recompute_pos):
    widened = hidden.astype(jnp.float32)
    inverse_rms = lax.rsqrt(lax.optimization_barrier(jnp.mean(widened * widened, axis=1, keepdims=True)) + 1e-05)
    normed = (widened * inverse_rms * norm_gain).astype(jnp.bfloat16)
    queries = lax.optimization_barrier(jnp.dot(normed, w_query, preferred_element_type=jnp.float32).astype(jnp.bfloat16))
    queries = queries.reshape(REQS, RT, KVH, GROUP, HD)
    keys_new = lax.optimization_barrier(jnp.dot(normed, w_key, preferred_element_type=jnp.float32).astype(jnp.bfloat16))
    values_new = lax.optimization_barrier(jnp.dot(normed, w_value, preferred_element_type=jnp.float32).astype(jnp.bfloat16))
    fresh = jnp.concatenate([keys_new.reshape(REQS, RT, KVH, HD), values_new.reshape(REQS, RT, KVH, HD)], axis=3)
    fresh = fresh.transpose(0, 2, 1, 3)
    prompt = sys_cache.transpose(1, 0, 2)
    offsets = jnp.arange(MAXP * PT, dtype=jnp.int32)
    scale = HD ** (-0.5)

    def one_request(items):
        ids, valid_count, positions, query_block, fresh_block = items
        stored = passage_cache[passage_place[ids]]
        context = stored.transpose(1, 0, 2, 3).reshape(KVH, MAXP * PT, 2 * HD)
        context = context.at[:, positions, :].set(fresh_block)
        keyvals = jnp.concatenate([prompt, context], axis=1)
        scores = jnp.einsum('rkgd,knd->kgrn', query_block.astype(jnp.float32), keyvals[:, :, :HD].astype(jnp.float32)) * scale
        allowed = (offsets[None, :] <= positions[:, None]) & (offsets[None, :] < valid_count * PT)
        allowed = jnp.concatenate([jnp.ones((RT, SYS), dtype=bool), allowed], axis=1)
        scores = jnp.where(allowed[None, None], scores, -1e+30)
        largest = lax.optimization_barrier(jnp.max(scores, axis=3, keepdims=True))
        weights = jnp.exp(scores - largest)
        total = lax.optimization_barrier(jnp.sum(weights, axis=3, keepdims=True))
        weights_low = lax.optimization_barrier(weights.astype(jnp.bfloat16)).astype(jnp.float32)
        mixed = jnp.einsum('kgrn,knd->kgrd', weights_low, keyvals[:, :, HD:].astype(jnp.float32))
        result = (mixed / total).astype(jnp.bfloat16)
        return result.transpose(2, 0, 1, 3).reshape(RT, KVH * GROUP * HD)
    attended = lax.map(one_request, (passage_ids, passage_count, recompute_pos, queries, fresh))
    return attended.reshape(TOKS, HQ * HD)
```

```python
import jax
import jax.numpy as jnp
from jax import lax
from jax.experimental import pallas as pl
from jax.experimental.pallas import tpu as pltpu
from jax.sharding import PartitionSpec as P

HD = 128
GROUP = 8
PT = 256
MAXP = 4
RT = 80
SIDE = 4
FEAT = 2048
REQ_DEV = 8
STORED = 8
CAP = 2
SLOTS = SIDE * CAP
SYS = 1024
SYS_DEV = 32
WT = 256
ROWS = GROUP * RT
HALF = ROWS // 2
FAR = 1 << 20
LOW = -1e30
EXP_SCALE = HD ** (-0.5) * 1.4426950408889634
MESH = pl.DeviceIdType.MESH


def kernel(
    hidden,
    gain,
    w_query,
    w_key,
    w_value,
    stored,
    sys_own,
    wish,
    spot,
    code,
    limit,
    out,
    weights,
    tokens,
    normed,
    along,
    along_sys,
    picked,
    held,
    held_sys,
    wishes,
    wishes_s,
    projected,
    part_mix,
    part_stat,
    z_send,
    z_recv,
    a_send,
    a_recv,
    as_send,
    as_recv,
    w_send,
    w_recv,
    b_send,
    b_recv,
    bs_send,
    bs_recv,
    local,
):
    z = lax.axis_index("store")
    req = lax.axis_index("req")
    x = req // 8
    y = lax.rem(req // 2, 4)
    c = lax.rem(req, 2)
    a_pos = x * (1 - c) + y * c
    b_pos = y * (1 - c) + x * c

    def at(xx, yy, cc):
        return (z, (lax.rem(xx, 4) * 4 + lax.rem(yy, 4)) * 2 + cc)

    def along_dev(d):
        return at(x + d * (1 - c), y + d * c, c)

    def asker(db, dc):
        cc = c if dc == 0 else 1 - c
        return at(x + db * c, y + db * (1 - c), cc)

    def via(e, dc):
        cc = c if dc == 0 else 1 - c
        return at(x + e * cc, y + e * (1 - cc), cc)

    def via_index(e, dc):
        cc = c if dc == 0 else 1 - c
        return cc * 4 + lax.rem(y * (1 - cc) + x * cc + e, 4)

    right = (lax.rem(z + 1, 4), req)
    left = (lax.rem(z + 3, 4), req)
    me_via = c * 4 + b_pos

    pieces = []
    for j in range(4):
        pieces.append((w_query.at[:, pl.ds(j * WT, WT)], weights.at[j]))
    pieces.append((w_key, weights.at[4, :, pl.ds(0, HD)]))
    pieces.append((w_value, weights.at[4, :, pl.ds(HD, HD)]))
    pieces.append((hidden, tokens.at[0]))
    pieces.append((stored, along.at[a_pos]))
    pieces.append((sys_own, along_sys.at[a_pos]))
    pieces.append((wish, wishes.at[0]))
    loads = [pltpu.make_async_copy(s, d, local.at[i]) for i, (s, d) in enumerate(pieces)]

    barrier = pltpu.get_barrier_semaphore()
    partners = [left, right, at(x, y, 1 - c)]
    for d in range(1, 4):
        for cc in range(2):
            partners.append(at(x + d, y, cc))
            partners.append(at(x, y + d, cc))
    for device in partners:
        pl.semaphore_signal(barrier, inc=1, device_id=device, device_id_type=MESH)
    for load in loads:
        load.start()
    pl.semaphore_wait(barrier, len(partners))

    def remote(src, dst, send, recv, device):
        return pltpu.make_async_remote_copy(
            src_ref=src,
            dst_ref=dst,
            send_sem=send,
            recv_sem=recv,
            device_id=device,
            device_id_type=MESH,
        )

    def rows_of(t):
        return pl.ds(pl.multiple_of(t * RT, 16), RT)

    def z_own(t, way):
        return remote(
            hidden.at[rows_of(t)],
            tokens.at[1 + way, rows_of(t)],
            z_send.at[way, t],
            z_recv.at[way, t],
            (right, left)[way],
        )

    def z_pass(t, way):
        cols = pl.ds(way * (FEAT // 2), FEAT // 2)
        return remote(
            tokens.at[1 + way, rows_of(t), cols],
            tokens.at[3, rows_of(t), cols],
            z_send.at[2 + way, t],
            z_recv.at[2 + way, t],
            (right, left)[way],
        )

    def a_copy(d, pos):
        return remote(stored, along.at[pos], a_send.at[d - 1], a_recv.at[d - 1], along_dev(d))

    def as_copy(d, pos):
        return remote(sys_own, along_sys.at[pos], as_send.at[d - 1], as_recv.at[d - 1], along_dev(d))

    def wish_copy(e, dc):
        slot = ((4 - e) % 4) * 2 + dc
        return remote(wish, wishes.at[slot], w_send.at[slot], w_recv.at[slot], via(e, dc))

    def b_copy(db, dc, index):
        q = db * 2 + dc
        return remote(picked.at[q], held.at[index], b_send.at[q], b_recv.at[q], asker(db, dc))

    def bs_copy(db, dc, index):
        q = db * 2 + dc
        return remote(along_sys, held_sys.at[index], bs_send.at[q], bs_recv.at[q], asker(db, dc))

    others = [(db, dc) for db in (1, 3, 2, 0) for dc in range(2) if (db, dc) != (0, 0)]

    for way in range(2):
        z_own(0, way).start()
    for db, dc in others:
        wish_copy((4 - db) % 4, dc).start()
    for d in (1, 3, 2):
        as_copy(d, a_pos).start()
    for d in (1, 3, 2):
        a_copy(d, a_pos).start()
    for way in range(2):
        z_own(1, way).start()
    for load in loads:
        load.wait()

    def fetch():
        for db, dc in others:
            wish_copy((4 - db) % 4, dc).wait_recv()
        copy = pltpu.make_async_copy(wishes, wishes_s, local.at[0])
        copy.start()
        for d in (1, 3, 2):
            as_copy(d, lax.rem(a_pos + 4 - d, 4)).wait_recv()
        for db, dc in others:
            bs_copy(db, dc, me_via).start()
        held_sys[me_via] = along_sys[...]
        copy.wait()
        for d in (1, 3, 2):
            a_copy(d, lax.rem(a_pos + 4 - d, 4)).wait_recv()
        for db, dc in others:
            q = db * 2 + dc

            def pick(k, _, q=q):
                row = wishes_s[q, me_via, k]
                picked[q, k] = along[k // CAP, row]
                return 0

            lax.fori_loop(0, SLOTS, pick, 0)
            b_copy(db, dc, me_via).start()

        def keep(k, _):
            row = wishes_s[0, me_via, k]
            held[me_via, k] = along[k // CAP, row]
            return 0

        lax.fori_loop(0, SLOTS, keep, 0)

    spread = (0, 3, 1, 2)

    def project(k):
        for step in range(2):
            for way in range(2):
                z_pass(2 * k + step, way).wait_recv()

        def norm(i, _):
            rows = pl.ds(pl.multiple_of(k * (2 * RT) + i * 16, 16), 16)
            total = jnp.zeros((16, 1), jnp.float32)
            for slot in range(4):
                wide = tokens[slot, rows, :].astype(jnp.float32)
                total = total + jnp.sum(wide * wide, axis=1, keepdims=True)
            inverse = lax.rsqrt(total * (1.0 / (4 * FEAT)) + 1e-05)
            to = pl.ds(pl.multiple_of(i * 16, 16), 16)
            for slot in range(4):
                source = lax.rem(z + spread[slot], 4)
                cols = pl.ds(pl.multiple_of(source * FEAT, FEAT), FEAT)
                wide = tokens[slot, rows, :].astype(jnp.float32)
                normed[source, to, :] = (wide * inverse * gain[:, cols]).astype(jnp.bfloat16)
            return 0

        lax.fori_loop(0, 2 * RT // 16, norm, 0)

        def tile(j, _):
            total = jnp.zeros((2 * RT, WT), jnp.float32)
            for source in range(4):
                total = total + jnp.dot(
                    normed[source],
                    weights[j, pl.ds(source * FEAT, FEAT), :],
                    preferred_element_type=jnp.float32,
                )
            low = total.astype(jnp.bfloat16)
            for half in range(2):
                for step in range(2):
                    to = pl.ds(pl.multiple_of((2 * j + half) * RT, 16), RT)
                    projected[2 * k + step, to, :] = low[
                        step * RT : (step + 1) * RT, half * HD : (half + 1) * HD
                    ]
            return 0

        lax.fori_loop(0, 5, tile, 0)

    def dot_t(a, b):
        return lax.dot_general(a, b, (((1,), (1,)), ((), ())), preferred_element_type=jnp.float32)

    def half_rows(hb):
        return pl.ds(pl.multiple_of(hb * HALF, 16), HALF)

    def shared(i, _):
        r = i // 2
        rows = half_rows(lax.rem(i, 2))
        query = projected[r, rows, :]
        keyvals = held_sys[...].reshape(SYS, 2 * HD)
        scores = dot_t(query, keyvals[:, :HD])
        largest = jnp.max(scores, axis=1, keepdims=True)
        part = jnp.exp2((scores - largest) * EXP_SCALE)
        total = jnp.sum(part, axis=1, keepdims=True)
        mix = jnp.dot(
            part.astype(jnp.bfloat16), keyvals[:, HD:], preferred_element_type=jnp.float32
        )
        slot = lax.rem(r, 4)
        part_mix[slot, rows, :] = mix
        lane = lax.broadcasted_iota(jnp.int32, (HALF, HD), 1)
        part_stat[slot, rows, :] = jnp.where(lane < HD // 2, largest, total)
        return 0

    def own(i, _):
        r = i // 2
        hb = lax.rem(i, 2)
        rows = half_rows(hb)
        slot = lax.rem(r, 4)
        query = projected[r, rows, :]
        allowed_to = jnp.concatenate([limit[r]] * (GROUP // 2), axis=0)
        codes = code[r]
        spots = [spot[r * MAXP + j] for j in range(MAXP)]
        scores = []
        for j in range(MAXP):
            keys = held[spots[j] // SLOTS, lax.rem(spots[j], SLOTS), :, pl.ds(0, HD)]
            allowed = codes[:, j * PT : (j + 1) * PT] <= allowed_to
            scores.append(jnp.where(allowed, dot_t(query, keys), LOW))
        keys = projected[r, pl.ds(ROWS, RT), :]
        allowed = codes[:, MAXP * PT : MAXP * PT + RT] <= allowed_to
        scores.append(jnp.where(allowed, dot_t(query, keys), LOW))
        stat = part_stat[slot, rows, :]
        sys_largest = stat[:, 0:1]
        sys_total = stat[:, HD // 2 : HD // 2 + 1]
        largest = sys_largest
        for one in scores:
            largest = jnp.maximum(largest, jnp.max(one, axis=1, keepdims=True))
        shrink = jnp.exp2((sys_largest - largest) * EXP_SCALE)
        total = sys_total * shrink
        mix = part_mix[slot, rows, :] * shrink
        for j in range(MAXP + 1):
            part = jnp.exp2((scores[j] - largest) * EXP_SCALE)
            total = total + jnp.sum(part, axis=1, keepdims=True)
            if j < MAXP:
                values = held[spots[j] // SLOTS, lax.rem(spots[j], SLOTS), :, pl.ds(HD, HD)]
            else:
                values = projected[r, pl.ds(ROWS + RT, RT), :]
            mix = mix + jnp.dot(
                part.astype(jnp.bfloat16), values, preferred_element_type=jnp.float32
            )
        result = (mix / total).astype(jnp.bfloat16)
        to = pl.ds(pl.multiple_of(r * RT, 16), RT)
        for h in range(GROUP // 2):
            cols = pl.ds(pl.multiple_of((hb * (GROUP // 2) + h) * HD, HD), HD)
            out[to, cols] = result[h * RT : (h + 1) * RT, :]
        return 0

    def step(t, _):
        @pl.when(t < 8)
        def _():
            for way in range(2):
                z_own(t, way).wait_recv()
                z_pass(t, way).start()

            @pl.when(t < 6)
            def _():
                for way in range(2):
                    z_own(t + 2, way).start()

        @pl.when(t == 1)
        def _():
            fetch()

        @pl.when(t == 3)
        def _():
            for db, dc in others:
                bs_copy(db, dc, via_index((4 - db) % 4, dc)).wait_recv()

        @pl.when((t == 3) | (t == 5) | (t >= 7))
        def _():
            k = (t - 2) // 2
            project(k)
            lax.fori_loop(4 * k, 4 * k + 4, shared, 0)

        @pl.when(t == 6)
        def _():
            for db, dc in others:
                b_copy(db, dc, via_index((4 - db) % 4, dc)).wait_recv()

        @pl.when(t >= 6)
        def _():
            begin = jnp.where(t == 6, 0, 4 * t - 20)
            end = 4 * t - 16
            lax.fori_loop(begin, end, own, 0)

        return 0

    lax.fori_loop(0, 9, step, 0)

    def finish(t, _):
        for way in range(2):
            z_own(t, way).wait_send()
            z_pass(t, way).wait_send()
        return 0

    lax.fori_loop(0, 8, finish, 0)
    for d in (1, 3, 2):
        a_copy(d, a_pos).wait_send()
        as_copy(d, a_pos).wait_send()
    for db, dc in others:
        wish_copy((4 - db) % 4, dc).wait_send()
        b_copy(db, dc, me_via).wait_send()
        bs_copy(db, dc, me_via).wait_send()


def tables(passage_place, passage_ids, passage_count, recompute_pos):
    slots = REQ_DEV * MAXP
    place = passage_place[passage_ids.reshape(slots)]
    valid = (jnp.arange(MAXP)[None, :] < passage_count[:, None]).reshape(slots)
    holder = place // STORED
    row = lax.rem(place, STORED)
    xs, ys, cs = holder // 8, lax.rem(holder // 2, 4), lax.rem(holder, 2)
    order = jnp.arange(slots)
    before = (order[None, :] < order[:, None]) & (holder[None, :] == holder[:, None]) & valid[None, :]
    rank = jnp.minimum(jnp.sum(before.astype(jnp.int32), axis=1), CAP - 1)
    through = cs * 4 + jnp.where(cs == 0, ys, xs)
    index = through * SLOTS + jnp.where(cs == 0, xs, ys) * CAP + rank
    cells = jnp.arange(8 * 128).reshape(8, 128)
    cell = through * 128 + lax.rem(index, SLOTS)
    wish = jnp.sum(
        jnp.where((cells[:, :, None] == cell[None, None, :]) & valid[None, None, :], row, 0), axis=2
    ).astype(jnp.int32)
    table = index.reshape(REQ_DEV, MAXP)
    spot = jnp.where(valid.reshape(REQ_DEV, MAXP), table, table[:, :1]).reshape(slots)
    span = MAXP * PT
    offsets = jnp.arange(span, dtype=jnp.int32)
    touched = jnp.any(recompute_pos[:, :, None] == offsets[None, None, :], axis=1)
    code = jnp.where(touched, FAR, offsets[None, :])
    code = jnp.concatenate(
        [code, recompute_pos, jnp.full((REQ_DEV, 128 - RT), FAR, jnp.int32)], axis=1
    )
    limit = jnp.minimum(recompute_pos, passage_count[:, None] * PT - 1)
    return (
        wish,
        spot.astype(jnp.int32),
        code.reshape(REQ_DEV, 1, span + 128).astype(jnp.int32),
        limit.reshape(REQ_DEV, RT, 1).astype(jnp.int32),
    )


def body(
    hidden,
    norm_gain,
    w_query,
    w_key,
    w_value,
    passage_cache,
    sys_cache,
    passage_place,
    passage_ids,
    passage_count,
    recompute_pos,
):
    wish, spot, code, limit = tables(passage_place, passage_ids, passage_count, recompute_pos)
    anywhere = pl.BlockSpec(memory_space=pl.ANY)
    vmem = pl.BlockSpec(memory_space=pltpu.VMEM)
    smem = pl.BlockSpec(memory_space=pltpu.SMEM)
    bf16 = jnp.bfloat16
    dma = pltpu.SemaphoreType.DMA
    return pl.pallas_call(
        kernel,
        out_shape=jax.ShapeDtypeStruct((REQ_DEV * RT, GROUP * HD), bf16),
        in_specs=[
            anywhere,
            vmem,
            anywhere,
            anywhere,
            anywhere,
            anywhere,
            vmem,
            vmem,
            smem,
            vmem,
            vmem,
        ],
        out_specs=vmem,
        scratch_shapes=[
            pltpu.VMEM((5, 4 * FEAT, WT), bf16),
            pltpu.VMEM((4, REQ_DEV * RT, FEAT), bf16),
            pltpu.VMEM((4, 2 * RT, FEAT), bf16),
            pltpu.VMEM((SIDE, STORED, PT, 2 * HD), bf16),
            pltpu.VMEM((SIDE, SYS_DEV, 2 * HD), bf16),
            pltpu.VMEM((8, SLOTS, PT, 2 * HD), bf16),
            pltpu.VMEM((8, SLOTS, PT, 2 * HD), bf16),
            pltpu.VMEM((8, SIDE, SYS_DEV, 2 * HD), bf16),
            pltpu.VMEM((8, 8, 128), jnp.int32),
            pltpu.SMEM((8, 8, 128), jnp.int32),
            pltpu.VMEM((REQ_DEV, 10 * RT, HD), bf16),
            pltpu.VMEM((4, ROWS, HD), jnp.float32),
            pltpu.VMEM((4, ROWS, HD), jnp.float32),
            dma((4, 8)),
            dma((4, 8)),
            dma((3,)),
            dma((3,)),
            dma((3,)),
            dma((3,)),
            dma((8,)),
            dma((8,)),
            dma((8,)),
            dma((8,)),
            dma((8,)),
            dma((8,)),
            dma((10,)),
        ],
        compiler_params=pltpu.CompilerParams(
            collective_id=0, has_side_effects=True, vmem_limit_bytes=64 * 1024 * 1024
        ),
    )(
        hidden,
        norm_gain.reshape(1, 4 * FEAT),
        w_query,
        w_key,
        w_value,
        passage_cache.reshape(STORED, PT, 2 * HD),
        sys_cache.reshape(SYS_DEV, 2 * HD),
        wish,
        spot,
        code,
        limit,
    )


def solution(mesh):
    placed = (
        P("req", "store"),
        P(),
        P(None, "store"),
        P(None, "store"),
        P(None, "store"),
        P("req", "store", None, None),
        P("req", "store", None),
        P(),
        P("req", None),
        P("req"),
        P("req", None),
    )
    return jax.shard_map(
        body, mesh=mesh, in_specs=placed, out_specs=P("req", "store"), check_vma=False
    )
```

```python
import jax
import jax.numpy as jnp
from jax import lax
from jax.experimental import pallas as pl
from jax.experimental.pallas import tpu as pltpu
from jax.sharding import PartitionSpec as P

HD = 128
GROUP = 8
PT = 256
MAXP = 4
RT = 80
SIDE = 4
FEAT = 2048
REQ_DEV = 8
STORED = 8
CAP = 2
SLOTS = SIDE * CAP
SYS = 1024
SYS_DEV = 32
WT = 256
ROWS = GROUP * RT
HALF = ROWS // 2
FAR = 1 << 20
LOW = -1e30
EXP_SCALE = HD ** (-0.5) * 1.4426950408889634
MESH = pl.DeviceIdType.MESH


def kernel(
    hidden,
    gain,
    w_query,
    w_key,
    w_value,
    stored,
    sys_own,
    place,
    ids,
    count,
    pos,
    out,
    weights,
    tokens,
    normed,
    along_own,
    along_one,
    along_two,
    along_three,
    along_sys,
    picked,
    held,
    held_sys,
    mine,
    mine_s,
    wishes,
    wishes_s,
    holder_s,
    spot,
    code,
    limit,
    projected,
    part_mix,
    part_stat,
    z_send,
    z_recv,
    a_send,
    a_recv,
    as_send,
    as_recv,
    w_send,
    w_recv,
    b_send,
    b_recv,
    bs_send,
    bs_recv,
    local,
):
    z = lax.axis_index("store")
    req = lax.axis_index("req")
    x = req // 8
    y = lax.rem(req // 2, 4)
    c = lax.rem(req, 2)
    a_pos = x * (1 - c) + y * c
    b_pos = y * (1 - c) + x * c

    def at(xx, yy, cc):
        return (z, (lax.rem(xx, 4) * 4 + lax.rem(yy, 4)) * 2 + cc)

    def along_dev(d):
        return at(x + d * (1 - c), y + d * c, c)

    def asker(db, dc):
        cc = c if dc == 0 else 1 - c
        return at(x + db * c, y + db * (1 - c), cc)

    def via(e, dc):
        cc = c if dc == 0 else 1 - c
        return at(x + e * cc, y + e * (1 - cc), cc)

    def via_index(e, dc):
        cc = c if dc == 0 else 1 - c
        return cc * 4 + lax.rem(y * (1 - cc) + x * cc + e, 4)

    right = (lax.rem(z + 1, 4), req)
    left = (lax.rem(z + 3, 4), req)
    me_via = c * 4 + b_pos
    along = (along_own, along_one, along_two, along_three)

    pieces = []
    for j in range(4):
        pieces.append((w_query.at[:, pl.ds(j * WT, WT)], weights.at[j]))
    pieces.append((w_key, weights.at[4, :, pl.ds(0, HD)]))
    pieces.append((w_value, weights.at[4, :, pl.ds(HD, HD)]))
    pieces.append((hidden, tokens.at[0]))
    pieces.append((stored, along_own))
    pieces.append((sys_own, along_sys.at[a_pos]))
    loads = [pltpu.make_async_copy(s, d, local.at[i]) for i, (s, d) in enumerate(pieces)]

    barrier = pltpu.get_barrier_semaphore()
    partners = [left, right, at(x, y, 1 - c)]
    for d in range(1, 4):
        for cc in range(2):
            partners.append(at(x + d, y, cc))
            partners.append(at(x, y + d, cc))
    for device in partners:
        pl.semaphore_signal(barrier, inc=1, device_id=device, device_id_type=MESH)
    for load in loads:
        load.start()
    pl.semaphore_wait(barrier, len(partners))

    def remote(src, dst, send, recv, device):
        return pltpu.make_async_remote_copy(
            src_ref=src,
            dst_ref=dst,
            send_sem=send,
            recv_sem=recv,
            device_id=device,
            device_id_type=MESH,
        )

    def rows_of(t):
        return pl.ds(pl.multiple_of(t * RT, 16), RT)

    def z_own(t, way):
        return remote(
            hidden.at[rows_of(t)],
            tokens.at[1 + way, rows_of(t)],
            z_send.at[way, t],
            z_recv.at[way, t],
            (right, left)[way],
        )

    def z_pass(t, way):
        cols = pl.ds(way * (FEAT // 2), FEAT // 2)
        return remote(
            tokens.at[1 + way, rows_of(t), cols],
            tokens.at[3, rows_of(t), cols],
            z_send.at[2 + way, t],
            z_recv.at[2 + way, t],
            (right, left)[way],
        )

    def a_copy(d):
        return remote(stored, along[d], a_send.at[d - 1], a_recv.at[d - 1], along_dev(d))

    def a_pass(d):
        part = pl.ds(0 if d == 1 else STORED // 2, STORED // 2)
        return remote(
            along[d].at[part], along_two.at[part], a_send.at[d], a_recv.at[d], along_dev(d)
        )

    def as_copy(d, at_pos):
        return remote(sys_own, along_sys.at[at_pos], as_send.at[d - 1], as_recv.at[d - 1], along_dev(d))

    def wish_copy(e, dc):
        slot = ((4 - e) % 4) * 2 + dc
        return remote(mine, wishes.at[slot - 1], w_send.at[slot], w_recv.at[slot], via(e, dc))

    def b_copy(db, dc, off, index):
        q = db * 2 + dc
        part = pl.ds(off * CAP, CAP)
        return remote(
            picked.at[q, part],
            held.at[index, part],
            b_send.at[q, off],
            b_recv.at[q, off],
            asker(db, dc),
        )

    def bs_copy(db, dc, index):
        q = db * 2 + dc
        return remote(along_sys, held_sys.at[index], bs_send.at[q], bs_recv.at[q], asker(db, dc))

    others = [(db, dc) for db in (1, 3, 2, 0) for dc in range(2) if (db, dc) != (0, 0)]

    for way in range(2):
        z_own(0, way).start()
    for d in (1, 3, 2):
        as_copy(d, a_pos).start()
    for d in (1, 3):
        a_copy(d).start()
    for way in range(2):
        z_own(1, way).start()

    cells = lax.broadcasted_iota(jnp.int32, (8, 128), 0) * 128 + lax.broadcasted_iota(
        jnp.int32, (8, 128), 1
    )

    def ask(i, wish):
        r = i // MAXP
        stands = place[ids[lax.rem(i, MAXP), r]]
        valid = lax.rem(i, MAXP) < count[r]
        holder = lax.div(stands, STORED)
        row = lax.rem(stands, STORED)
        hx, hy, hc = lax.div(holder, 8), lax.rem(lax.div(holder, 2), 4), lax.rem(holder, 2)
        rank = 0
        for j in range(REQ_DEV * MAXP):
            rank = rank + jnp.where(holder_s[j] == holder, 1, 0)
        rank = jnp.minimum(rank, CAP - 1)
        holder_s[i] = jnp.where(valid, holder, -1)
        through = hc * 4 + hy * (1 - hc) + hx * hc
        ahead = (hx - x + 4) * (1 - hc) + (hy - y + 4) * hc
        which = lax.rem(ahead, 4) * CAP + rank
        spot[i] = jnp.where(valid, through * SLOTS + which, spot[r * MAXP])
        cell = jnp.where(valid, through * 128 + which, -1)
        return jnp.where(cells == cell, row, wish)

    for i in range(REQ_DEV * MAXP):
        holder_s[i] = -1
        spot[i] = 0
    mine[...] = lax.fori_loop(0, REQ_DEV * MAXP, ask, jnp.zeros((8, 128), jnp.int32))
    for db, dc in others:
        wish_copy((4 - db) % 4, dc).start()

    def mark(r, _):
        line = pos[pl.ds(r, 1), :]
        wide = jnp.broadcast_to(line, (RT, RT))
        eye = lax.broadcasted_iota(jnp.int32, (RT, RT), 0) == lax.broadcasted_iota(
            jnp.int32, (RT, RT), 1
        )
        column = jnp.sum(jnp.where(eye, wide, 0), axis=1, keepdims=True)
        limit[r] = jnp.minimum(column, count[r] * PT - 1)
        offsets = lax.broadcasted_iota(jnp.int32, (RT, MAXP * PT), 1)
        touched = jnp.max(jnp.where(offsets == column, FAR, 0), axis=0, keepdims=True)
        code[r, :, pl.ds(0, MAXP * PT)] = jnp.maximum(touched, offsets[0:1, :])
        code[r, :, pl.ds(MAXP * PT, RT)] = line
        return 0

    lax.fori_loop(0, REQ_DEV, mark, 0)

    def give(off):
        rows = along[(4 - off) % 4]
        for db, dc in others + [(0, 0)]:
            q = db * 2 + dc
            for rank in range(CAP):
                k = off * CAP + rank
                row = wishes_s[q - 1, me_via, k] if q else mine_s[me_via, k]
                if q:
                    picked[q, k] = rows[row]
                else:
                    held[me_via, k] = rows[row]
            if q:
                b_copy(db, dc, off, me_via).start()

    def give_own():
        for load in loads:
            load.wait()
        for d in (1, 3, 2):
            as_copy(d, lax.rem(a_pos + 4 - d, 4)).wait_recv()
        for db, dc in others:
            bs_copy(db, dc, me_via).start()
        held_sys[me_via] = along_sys[...]
        for db, dc in others:
            wish_copy((4 - db) % 4, dc).wait_recv()
        for source, target in ((wishes, wishes_s), (mine, mine_s)):
            copy = pltpu.make_async_copy(source, target, local.at[0])
            copy.start()
            copy.wait()
        give(0)

    def give_near():
        for d in (1, 3):
            a_copy(d).wait_recv()
            a_pass(d).start()
        give(3)
        give(1)

    def give_far():
        for d in (1, 3):
            a_pass(d).wait_recv()
        give(2)

    spread = (0, 3, 1, 2)

    def project(k):
        for step in range(2):
            for way in range(2):
                z_pass(2 * k + step, way).wait_recv()

        def norm(i, _):
            rows = pl.ds(pl.multiple_of(k * (2 * RT) + i * 16, 16), 16)
            total = jnp.zeros((16, 1), jnp.float32)
            for slot in range(4):
                wide = tokens[slot, rows, :].astype(jnp.float32)
                total = total + jnp.sum(wide * wide, axis=1, keepdims=True)
            inverse = lax.rsqrt(total * (1.0 / (4 * FEAT)) + 1e-05)
            to = pl.ds(pl.multiple_of(i * 16, 16), 16)
            for slot in range(4):
                source = lax.rem(z + spread[slot], 4)
                cols = pl.ds(pl.multiple_of(source * FEAT, FEAT), FEAT)
                wide = tokens[slot, rows, :].astype(jnp.float32)
                normed[source, to, :] = (wide * inverse * gain[:, cols]).astype(jnp.bfloat16)
            return 0

        lax.fori_loop(0, 2 * RT // 16, norm, 0)

        def tile(j, _):
            total = jnp.zeros((2 * RT, WT), jnp.float32)
            for source in range(4):
                total = total + jnp.dot(
                    normed[source],
                    weights[j, pl.ds(source * FEAT, FEAT), :],
                    preferred_element_type=jnp.float32,
                )
            low = total.astype(jnp.bfloat16)
            for half in range(2):
                for step in range(2):
                    to = pl.ds(pl.multiple_of((2 * j + half) * RT, 16), RT)
                    projected[2 * k + step, to, :] = low[
                        step * RT : (step + 1) * RT, half * HD : (half + 1) * HD
                    ]
            return 0

        lax.fori_loop(0, 5, tile, 0)

    def dot_t(a, b):
        return lax.dot_general(a, b, (((1,), (1,)), ((), ())), preferred_element_type=jnp.float32)

    def half_rows(hb):
        return pl.ds(pl.multiple_of(hb * HALF, 16), HALF)

    def shared(i, _):
        r = i // 2
        rows = half_rows(lax.rem(i, 2))
        query = projected[r, rows, :]
        keyvals = held_sys[...].reshape(SYS, 2 * HD)
        scores = dot_t(query, keyvals[:, :HD])
        largest = jnp.max(scores, axis=1, keepdims=True)
        part = jnp.exp2((scores - largest) * EXP_SCALE)
        total = jnp.sum(part, axis=1, keepdims=True)
        mix = jnp.dot(
            part.astype(jnp.bfloat16), keyvals[:, HD:], preferred_element_type=jnp.float32
        )
        slot = lax.rem(r, 4)
        part_mix[slot, rows, :] = mix
        lane = lax.broadcasted_iota(jnp.int32, (HALF, HD), 1)
        part_stat[slot, rows, :] = jnp.where(lane < HD // 2, largest, total)
        return 0

    def own(i, _):
        r = i // 2
        hb = lax.rem(i, 2)
        rows = half_rows(hb)
        slot = lax.rem(r, 4)
        query = projected[r, rows, :]
        allowed_to = jnp.concatenate([limit[r]] * (GROUP // 2), axis=0)
        codes = code[r]
        spots = [spot[r * MAXP + j] for j in range(MAXP)]
        scores = []
        for j in range(MAXP):
            keys = held[spots[j] // SLOTS, lax.rem(spots[j], SLOTS), :, pl.ds(0, HD)]
            allowed = codes[:, j * PT : (j + 1) * PT] <= allowed_to
            scores.append(jnp.where(allowed, dot_t(query, keys), LOW))
        keys = projected[r, pl.ds(ROWS, RT), :]
        allowed = codes[:, MAXP * PT : MAXP * PT + RT] <= allowed_to
        scores.append(jnp.where(allowed, dot_t(query, keys), LOW))
        stat = part_stat[slot, rows, :]
        sys_largest = stat[:, 0:1]
        sys_total = stat[:, HD // 2 : HD // 2 + 1]
        largest = sys_largest
        for one in scores:
            largest = jnp.maximum(largest, jnp.max(one, axis=1, keepdims=True))
        shrink = jnp.exp2((sys_largest - largest) * EXP_SCALE)
        total = sys_total * shrink
        mix = part_mix[slot, rows, :] * shrink
        for j in range(MAXP + 1):
            part = jnp.exp2((scores[j] - largest) * EXP_SCALE)
            total = total + jnp.sum(part, axis=1, keepdims=True)
            if j < MAXP:
                values = held[spots[j] // SLOTS, lax.rem(spots[j], SLOTS), :, pl.ds(HD, HD)]
            else:
                values = projected[r, pl.ds(ROWS + RT, RT), :]
            mix = mix + jnp.dot(
                part.astype(jnp.bfloat16), values, preferred_element_type=jnp.float32
            )
        result = (mix / total).astype(jnp.bfloat16)
        to = pl.ds(pl.multiple_of(r * RT, 16), RT)
        for h in range(GROUP // 2):
            cols = pl.ds(pl.multiple_of((hb * (GROUP // 2) + h) * HD, HD), HD)
            out[to, cols] = result[h * RT : (h + 1) * RT, :]
        return 0

    def step(t, _):
        @pl.when(t < 8)
        def _():
            for way in range(2):
                z_own(t, way).wait_recv()
                z_pass(t, way).start()

            @pl.when(t < 6)
            def _():
                for way in range(2):
                    z_own(t + 2, way).start()

        @pl.when(t == 0)
        def _():
            give_own()

        @pl.when(t == 1)
        def _():
            give_near()

        @pl.when(t == 2)
        def _():
            give_far()

        @pl.when(t == 3)
        def _():
            for db, dc in others:
                bs_copy(db, dc, via_index((4 - db) % 4, dc)).wait_recv()

        @pl.when((t == 3) | (t == 5) | (t >= 7))
        def _():
            k = (t - 2) // 2
            project(k)
            lax.fori_loop(4 * k, 4 * k + 4, shared, 0)

        @pl.when(t == 6)
        def _():
            for db, dc in others:
                for off in range(SIDE):
                    b_copy(db, dc, off, via_index((4 - db) % 4, dc)).wait_recv()

        @pl.when(t >= 6)
        def _():
            begin = jnp.where(t == 6, 0, 4 * t - 20)
            end = 4 * t - 16
            lax.fori_loop(begin, end, own, 0)

        return 0

    lax.fori_loop(0, 9, step, 0)

    def finish(t, _):
        for way in range(2):
            z_own(t, way).wait_send()
            z_pass(t, way).wait_send()
        return 0

    lax.fori_loop(0, 8, finish, 0)
    for d in (1, 3):
        a_copy(d).wait_send()
        a_pass(d).wait_send()
    for d in (1, 3, 2):
        as_copy(d, a_pos).wait_send()
    for db, dc in others:
        wish_copy((4 - db) % 4, dc).wait_send()
        for off in range(SIDE):
            b_copy(db, dc, off, me_via).wait_send()
        bs_copy(db, dc, me_via).wait_send()


def body(
    hidden,
    norm_gain,
    w_query,
    w_key,
    w_value,
    passage_cache,
    sys_cache,
    passage_place,
    passage_ids,
    passage_count,
    recompute_pos,
):
    anywhere = pl.BlockSpec(memory_space=pl.ANY)
    vmem = pl.BlockSpec(memory_space=pltpu.VMEM)
    smem = pl.BlockSpec(memory_space=pltpu.SMEM)
    bf16 = jnp.bfloat16
    dma = pltpu.SemaphoreType.DMA
    return pl.pallas_call(
        kernel,
        out_shape=jax.ShapeDtypeStruct((REQ_DEV * RT, GROUP * HD), bf16),
        in_specs=[
            anywhere,
            vmem,
            anywhere,
            anywhere,
            anywhere,
            anywhere,
            vmem,
            smem,
            smem,
            smem,
            vmem,
        ],
        out_specs=vmem,
        scratch_shapes=[
            pltpu.VMEM((5, 4 * FEAT, WT), bf16),
            pltpu.VMEM((4, REQ_DEV * RT, FEAT), bf16),
            pltpu.VMEM((4, 2 * RT, FEAT), bf16),
            pltpu.VMEM((STORED, PT, 2 * HD), bf16),
            pltpu.VMEM((STORED, PT, 2 * HD), bf16),
            pltpu.VMEM((STORED, PT, 2 * HD), bf16),
            pltpu.VMEM((STORED, PT, 2 * HD), bf16),
            pltpu.VMEM((SIDE, SYS_DEV, 2 * HD), bf16),
            pltpu.VMEM((8, SLOTS, PT, 2 * HD), bf16),
            pltpu.VMEM((8, SLOTS, PT, 2 * HD), bf16),
            pltpu.VMEM((8, SIDE, SYS_DEV, 2 * HD), bf16),
            pltpu.VMEM((8, 128), jnp.int32),
            pltpu.SMEM((8, 128), jnp.int32),
            pltpu.VMEM((7, 8, 128), jnp.int32),
            pltpu.SMEM((7, 8, 128), jnp.int32),
            pltpu.SMEM((REQ_DEV * MAXP,), jnp.int32),
            pltpu.SMEM((REQ_DEV * MAXP,), jnp.int32),
            pltpu.VMEM((REQ_DEV, 1, MAXP * PT + 128), jnp.int32),
            pltpu.VMEM((REQ_DEV, RT, 1), jnp.int32),
            pltpu.VMEM((REQ_DEV, 10 * RT, HD), bf16),
            pltpu.VMEM((4, ROWS, HD), jnp.float32),
            pltpu.VMEM((4, ROWS, HD), jnp.float32),
            dma((4, 8)),
            dma((4, 8)),
            dma((4,)),
            dma((4,)),
            dma((3,)),
            dma((3,)),
            dma((8,)),
            dma((8,)),
            dma((8, SIDE)),
            dma((8, SIDE)),
            dma((8,)),
            dma((8,)),
            dma((9,)),
        ],
        compiler_params=pltpu.CompilerParams(
            collective_id=0, has_side_effects=True, vmem_limit_bytes=64 * 1024 * 1024
        ),
    )(
        hidden,
        norm_gain.reshape(1, 4 * FEAT),
        w_query,
        w_key,
        w_value,
        passage_cache.reshape(STORED, PT, 2 * HD),
        sys_cache.reshape(SYS_DEV, 2 * HD),
        passage_place,
        passage_ids.T,
        passage_count,
        recompute_pos,
    )


def solution(mesh):
    placed = (
        P("req", "store"),
        P(),
        P(None, "store"),
        P(None, "store"),
        P(None, "store"),
        P("req", "store", None, None),
        P("req", "store", None),
        P(),
        P("req", None),
        P("req"),
        P("req", None),
    )
    return jax.shard_map(
        body, mesh=mesh, in_specs=placed, out_specs=P("req", "store"), check_vma=False
    )
```

```python
import jax
import jax.numpy as jnp
from jax import lax
from jax.experimental import pallas as pl
from jax.experimental.pallas import tpu as pltpu
from jax.sharding import PartitionSpec as P

HD = 128
GROUP = 8
PT = 256
MAXP = 4
RT = 80
SIDE = 4
FEAT = 2048
REQ_DEV = 8
STORED = 8
CAP = 2
SLOTS = SIDE * CAP
SYS = 1024
SYS_DEV = 32
WT = 256
ROWS = GROUP * RT
HALF = ROWS // 2
FAR = 1 << 20
LOW = -1e30
EXP_SCALE = HD ** (-0.5) * 1.4426950408889634
MESH = pl.DeviceIdType.MESH


def kernel(
    hidden,
    gain,
    w_query,
    w_key,
    w_value,
    stored,
    sys_own,
    place,
    ids,
    count,
    pos,
    out,
    weights,
    tokens,
    normed,
    along_own,
    along_one,
    along_two,
    along_three,
    along_sys,
    picked,
    held,
    held_sys,
    mine,
    mine_s,
    wishes,
    wishes_s,
    holder_s,
    spot,
    projected,
    part_mix,
    part_stat,
    partial,
    square_own,
    square_in,
    inverse,
    bias,
    z_send,
    z_recv,
    q_send,
    q_recv,
    a_send,
    a_recv,
    as_send,
    as_recv,
    w_send,
    w_recv,
    b_send,
    b_recv,
    bs_send,
    bs_recv,
    local,
):
    z = lax.axis_index("store")
    req = lax.axis_index("req")
    x = req // 8
    y = lax.rem(req // 2, 4)
    c = lax.rem(req, 2)
    a_pos = x * (1 - c) + y * c
    b_pos = y * (1 - c) + x * c

    def at(xx, yy, cc):
        return (z, (lax.rem(xx, 4) * 4 + lax.rem(yy, 4)) * 2 + cc)

    def along_dev(d):
        return at(x + d * (1 - c), y + d * c, c)

    def asker(db, dc):
        cc = c if dc == 0 else 1 - c
        return at(x + db * c, y + db * (1 - c), cc)

    def via(e, dc):
        cc = c if dc == 0 else 1 - c
        return at(x + e * cc, y + e * (1 - cc), cc)

    def via_index(e, dc):
        cc = c if dc == 0 else 1 - c
        return cc * 4 + lax.rem(y * (1 - cc) + x * cc + e, 4)

    right = (lax.rem(z + 1, 4), req)
    left = (lax.rem(z + 3, 4), req)
    me_via = c * 4 + b_pos
    along = (along_own, along_one, along_two, along_three)

    pieces = []
    for j in range(4):
        pieces.append((w_query.at[:, pl.ds(j * WT, WT)], weights.at[j]))
    pieces.append((w_key, weights.at[4, :, pl.ds(0, HD)]))
    pieces.append((w_value, weights.at[4, :, pl.ds(HD, HD)]))
    pieces.append((hidden, tokens.at[0]))
    pieces.append((stored, along_own))
    pieces.append((sys_own, along_sys.at[a_pos]))
    loads = [pltpu.make_async_copy(s, d, local.at[i]) for i, (s, d) in enumerate(pieces)]

    barrier = pltpu.get_barrier_semaphore()
    opposite = (lax.rem(z + 2, 4), req)
    partners = [left, right, opposite, at(x, y, 1 - c)]
    for d in range(1, 4):
        for cc in range(2):
            partners.append(at(x + d, y, cc))
            partners.append(at(x, y + d, cc))
    for device in partners:
        pl.semaphore_signal(barrier, inc=1, device_id=device, device_id_type=MESH)
    for load in loads[-3:]:
        load.start()
    pl.semaphore_wait(barrier, len(partners))

    def remote(src, dst, send, recv, device):
        return pltpu.make_async_remote_copy(
            src_ref=src,
            dst_ref=dst,
            send_sem=send,
            recv_sem=recv,
            device_id=device,
            device_id_type=MESH,
        )

    def rows_of(t):
        return pl.ds(pl.multiple_of(t * RT, 16), RT)

    def z_own(t, way):
        return remote(
            hidden.at[rows_of(t)],
            tokens.at[1 + way, rows_of(t)],
            z_send.at[way, t],
            z_recv.at[way, t],
            (right, left)[way],
        )

    def z_pass(t, way):
        cols = pl.ds(way * (FEAT // 2), FEAT // 2)
        return remote(
            tokens.at[1 + way, rows_of(t), cols],
            tokens.at[3, rows_of(t), cols],
            z_send.at[2 + way, t],
            z_recv.at[2 + way, t],
            (right, left)[way],
        )

    def a_copy(d):
        return remote(stored, along[d], a_send.at[d - 1], a_recv.at[d - 1], along_dev(d))

    def a_pass(d):
        part = pl.ds(0 if d == 1 else STORED // 2, STORED // 2)
        return remote(
            along[d].at[part], along_two.at[part], a_send.at[d], a_recv.at[d], along_dev(d)
        )

    def as_copy(d, at_pos):
        return remote(sys_own, along_sys.at[at_pos], as_send.at[d - 1], as_recv.at[d - 1], along_dev(d))

    def wish_copy(e, dc):
        slot = ((4 - e) % 4) * 2 + dc
        return remote(mine, wishes.at[slot - 1], w_send.at[slot], w_recv.at[slot], via(e, dc))

    def b_copy(db, dc, off, index):
        q = db * 2 + dc
        part = pl.ds(off * CAP, CAP)
        return remote(
            picked.at[q, part],
            held.at[index, part],
            b_send.at[q, off],
            b_recv.at[q, off],
            asker(db, dc),
        )

    def bs_copy(db, dc, index):
        q = db * 2 + dc
        return remote(along_sys, held_sys.at[index], bs_send.at[q], bs_recv.at[q], asker(db, dc))

    others = [(db, dc) for db in (1, 3, 2, 0) for dc in range(2) if (db, dc) != (0, 0)]

    for way in range(2):
        z_own(0, way).start()
    for d in (1, 3, 2):
        as_copy(d, a_pos).start()
    for d in (1, 3):
        a_copy(d).start()
    for way in range(2):
        z_own(1, way).start()

    cells = lax.broadcasted_iota(jnp.int32, (8, 128), 0) * 128 + lax.broadcasted_iota(
        jnp.int32, (8, 128), 1
    )

    def ask(i, wish):
        r = i // MAXP
        stands = place[ids[lax.rem(i, MAXP), r]]
        valid = lax.rem(i, MAXP) < count[r]
        holder = lax.div(stands, STORED)
        row = lax.rem(stands, STORED)
        hx, hy, hc = lax.div(holder, 8), lax.rem(lax.div(holder, 2), 4), lax.rem(holder, 2)
        rank = 0
        for j in range(REQ_DEV * MAXP):
            rank = rank + jnp.where(holder_s[j] == holder, 1, 0)
        rank = jnp.minimum(rank, CAP - 1)
        holder_s[i] = jnp.where(valid, holder, -1)
        through = hc * 4 + hy * (1 - hc) + hx * hc
        ahead = (hx - x + 4) * (1 - hc) + (hy - y + 4) * hc
        which = lax.rem(ahead, 4) * CAP + rank
        spot[i] = jnp.where(valid, through * SLOTS + which, spot[r * MAXP])
        cell = jnp.where(valid, through * 128 + which, -1)
        return jnp.where(cells == cell, row, wish)

    for i in range(REQ_DEV * MAXP):
        holder_s[i] = -1
        spot[i] = 0
    mine[...] = lax.fori_loop(0, REQ_DEV * MAXP, ask, jnp.zeros((8, 128), jnp.int32))
    for db, dc in others:
        wish_copy((4 - db) % 4, dc).start()

    eye = lax.broadcasted_iota(jnp.int32, (RT, RT), 0) == lax.broadcasted_iota(
        jnp.int32, (RT, RT), 1
    )

    def square_copy(d):
        device = (right, opposite, left)[d - 1]
        return remote(square_own, square_in.at[d - 1], q_send.at[d - 1], q_recv.at[d - 1], device)

    def square(t, _):
        column = jnp.zeros((RT, 1), jnp.float32)
        for part in range(FEAT // 256):
            wide = tokens[0, rows_of(t), pl.ds(part * 256, 256)].astype(jnp.float32)
            column = column + jnp.sum(wide * wide, axis=1, keepdims=True)
        square_own[pl.ds(t, 1), pl.ds(0, RT)] = jnp.sum(
            jnp.where(eye, column, 0.0), axis=0, keepdims=True
        )
        return 0

    square_own[...] = jnp.zeros((8, 128), jnp.float32)
    loads[-3].wait()
    lax.fori_loop(0, 8, square, 0)
    for d in (1, 3, 2):
        square_copy(d).start()

    def invert(t, _):
        line = square_own[pl.ds(t, 1), pl.ds(0, RT)]
        for d in range(3):
            line = line + square_in[d, pl.ds(t, 1), pl.ds(0, RT)]
        line = lax.rsqrt(line * (1.0 / (4 * FEAT)) + 1e-05)
        inverse[rows_of(t), :] = jnp.sum(
            jnp.where(eye, jnp.broadcast_to(line, (RT, RT)), 0.0), axis=1, keepdims=True
        )
        return 0

    def mark(r):
        line = pos[pl.ds(r, 1), :]
        wide = jnp.broadcast_to(line, (RT, RT))
        column = jnp.sum(jnp.where(eye, wide, 0), axis=1, keepdims=True)
        limit = jnp.minimum(column, count[r] * PT - 1)
        offsets = lax.broadcasted_iota(jnp.int32, (RT, MAXP * PT), 1)
        touched = jnp.max(jnp.where(offsets == column, FAR, 0), axis=0, keepdims=True)
        stored_code = jnp.maximum(jnp.broadcast_to(touched, offsets.shape), offsets)
        bias[:, pl.ds(0, MAXP * PT)] = jnp.where(stored_code <= limit, 0.0, LOW)
        bias[:, pl.ds(MAXP * PT, RT)] = jnp.where(wide <= limit, 0.0, LOW)

    def give(off):
        rows = along[(4 - off) % 4]
        for db, dc in others + [(0, 0)]:
            q = db * 2 + dc
            for rank in range(CAP):
                k = off * CAP + rank
                row = wishes_s[q - 1, me_via, k] if q else mine_s[me_via, k]
                if q:
                    picked[q, k] = rows[row]
                else:
                    held[me_via, k] = rows[row]
            if q:
                b_copy(db, dc, off, me_via).start()

    def give_own():
        for load in loads[-2:]:
            load.wait()
        for d in (1, 3, 2):
            as_copy(d, lax.rem(a_pos + 4 - d, 4)).wait_recv()
        for db, dc in others:
            bs_copy(db, dc, me_via).start()
        held_sys[me_via] = along_sys[...]
        for db, dc in others:
            wish_copy((4 - db) % 4, dc).wait_recv()
        for source, target in ((wishes, wishes_s), (mine, mine_s)):
            copy = pltpu.make_async_copy(source, target, local.at[0])
            copy.start()
            copy.wait()
        give(0)

    def give_near():
        for d in (1, 3):
            a_copy(d).wait_recv()
            a_pass(d).start()
        give(3)
        give(1)

    def give_far():
        for d in (1, 3):
            a_pass(d).wait_recv()
        give(2)

    spread = (0, 3, 1, 2)

    def scale(k, slots):
        def norm(i, _):
            rows = pl.ds(pl.multiple_of(k * (2 * RT) + i * 16, 16), 16)
            to = pl.ds(pl.multiple_of(i * 16, 16), 16)
            for slot in slots:
                source = lax.rem(z + spread[slot], 4)
                cols = pl.ds(pl.multiple_of(source * FEAT, FEAT), FEAT)
                wide = tokens[slot, rows, :].astype(jnp.float32)
                normed[slot, to, :] = (wide * inverse[rows, :] * gain[:, cols]).astype(jnp.bfloat16)
            return 0

        lax.fori_loop(0, 2 * RT // 16, norm, 0)

    def product(j, slot):
        source = lax.rem(z + spread[slot], 4)
        rows = pl.ds(pl.multiple_of(source * FEAT, FEAT), FEAT)
        return jnp.dot(normed[slot], weights[j, rows, :], preferred_element_type=jnp.float32)

    def project_near(k):
        scale(k, (0, 1, 2))

        def tile(j, _):
            partial[j] = product(j, 0) + product(j, 1) + product(j, 2)
            return 0

        lax.fori_loop(0, 5, tile, 0)

    def project_far(k):
        for step in range(2):
            for way in range(2):
                z_pass(2 * k + step, way).wait_recv()
        scale(k, (3,))

        def tile(j, _):
            low = (partial[j] + product(j, 3)).astype(jnp.bfloat16)
            for half in range(2):
                for step in range(2):
                    to = pl.ds(pl.multiple_of((2 * j + half) * RT, 16), RT)
                    projected[2 * k + step, to, :] = low[
                        step * RT : (step + 1) * RT, half * HD : (half + 1) * HD
                    ]
            return 0

        lax.fori_loop(0, 5, tile, 0)

    def dot_t(a, b):
        return lax.dot_general(a, b, (((1,), (1,)), ((), ())), preferred_element_type=jnp.float32)

    def half_rows(hb):
        return pl.ds(hb * HALF, HALF)

    def shared(r, _):
        for hb in range(2):
            shared_half(r, hb)
        return 0

    def shared_half(r, hb):
        rows = half_rows(hb)
        query = projected[r, rows, :]
        keyvals = held_sys[...].reshape(SYS, 2 * HD)
        scores = dot_t(query, keyvals[:, :HD])
        largest = jnp.max(scores, axis=1, keepdims=True)
        part = jnp.exp2((scores - largest) * EXP_SCALE)
        total = jnp.sum(part, axis=1, keepdims=True)
        mix = jnp.dot(
            part.astype(jnp.bfloat16), keyvals[:, HD:], preferred_element_type=jnp.float32
        )
        slot = lax.rem(r, 6)
        part_mix[slot, rows, :] = mix
        lane = lax.broadcasted_iota(jnp.int32, (HALF, HD), 1)
        part_stat[slot, rows, :] = jnp.where(lane < HD // 2, largest, total)

    def own(r, _):
        mark(r)
        for hb in range(2):
            own_half(r, hb)
        return 0

    def own_half(r, hb):
        rows = half_rows(hb)
        slot = lax.rem(r, 6)
        query = projected[r, rows, :]

        def masked(one, first, width):
            hide = bias[:, pl.ds(first, width)]
            return one + jnp.concatenate([hide] * (GROUP // 2), axis=0)

        spots = [spot[r * MAXP + j] for j in range(MAXP)]
        scores = []
        for j in range(MAXP):
            keys = held[spots[j] // SLOTS, lax.rem(spots[j], SLOTS), :, pl.ds(0, HD)]
            scores.append(masked(dot_t(query, keys), j * PT, PT))
        keys = projected[r, pl.ds(ROWS, RT), :]
        scores.append(masked(dot_t(query, keys), MAXP * PT, RT))
        stat = part_stat[slot, rows, :]
        sys_largest = stat[:, 0:1]
        sys_total = stat[:, HD // 2 : HD // 2 + 1]
        largest = sys_largest
        for one in scores:
            largest = jnp.maximum(largest, jnp.max(one, axis=1, keepdims=True))
        shrink = jnp.exp2((sys_largest - largest) * EXP_SCALE)
        total = sys_total * shrink
        mix = part_mix[slot, rows, :] * shrink
        for j in range(MAXP + 1):
            part = jnp.exp2((scores[j] - largest) * EXP_SCALE)
            total = total + jnp.sum(part, axis=1, keepdims=True)
            if j < MAXP:
                values = held[spots[j] // SLOTS, lax.rem(spots[j], SLOTS), :, pl.ds(HD, HD)]
            else:
                values = projected[r, pl.ds(ROWS + RT, RT), :]
            mix = mix + jnp.dot(
                part.astype(jnp.bfloat16), values, preferred_element_type=jnp.float32
            )
        result = (mix / total).astype(jnp.bfloat16)
        to = pl.ds(pl.multiple_of(r * RT, 16), RT)
        for h in range(GROUP // 2):
            cols = pl.ds((hb * (GROUP // 2) + h) * HD, HD)
            out[to, cols] = result[h * RT : (h + 1) * RT, :]

    def step(t, _):
        @pl.when(t < 8)
        def _():
            for way in range(2):
                z_own(t, way).wait_recv()
                z_pass(t, way).start()

            @pl.when(t < 6)
            def _():
                for way in range(2):
                    z_own(t + 2, way).start()

        @pl.when(t == 0)
        def _():
            give_own()
            loads[0].start()
            loads[1].start()

        @pl.when(t == 1)
        def _():
            give_near()
            for load in loads[2:4]:
                load.start()

        @pl.when(t == 2)
        def _():
            give_far()
            for load in loads[4:-3]:
                load.start()
            for d in (1, 3, 2):
                square_copy(d).wait_recv()
            lax.fori_loop(0, 8, invert, 0)
            for load in loads[:-3]:
                load.wait()

        @pl.when(t == 3)
        def _():
            for db, dc in others:
                bs_copy(db, dc, via_index((4 - db) % 4, dc)).wait_recv()

        @pl.when((t == 3) | (t == 4) | (t == 6) | (t == 7))
        def _():
            project_near(jnp.where(t > 4, t - 4, t - 3))

        @pl.when((t == 3) | (t == 5) | (t == 6) | (t == 8))
        def _():
            k = (t - 2) // 2
            project_far(k)
            lax.fori_loop(2 * k, 2 * k + 2, shared, 0)

        @pl.when(t == 6)
        def _():
            for db, dc in others:
                for off in range(SIDE):
                    b_copy(db, dc, off, via_index((4 - db) % 4, dc)).wait_recv()

        @pl.when(t >= 6)
        def _():
            begin = jnp.where(t == 6, 0, 4 * t - 26)
            end = jnp.where(t == 6, 2, 2 * t - 8)
            lax.fori_loop(begin, end, own, 0)

        return 0

    lax.fori_loop(0, 9, step, 0)

    def finish(t, _):
        for way in range(2):
            z_own(t, way).wait_send()
            z_pass(t, way).wait_send()
        return 0

    lax.fori_loop(0, 8, finish, 0)
    for d in (1, 3, 2):
        square_copy(d).wait_send()
    for d in (1, 3):
        a_copy(d).wait_send()
        a_pass(d).wait_send()
    for d in (1, 3, 2):
        as_copy(d, a_pos).wait_send()
    for db, dc in others:
        wish_copy((4 - db) % 4, dc).wait_send()
        for off in range(SIDE):
            b_copy(db, dc, off, me_via).wait_send()
        bs_copy(db, dc, me_via).wait_send()


def body(
    hidden,
    norm_gain,
    w_query,
    w_key,
    w_value,
    passage_cache,
    sys_cache,
    passage_place,
    passage_ids,
    passage_count,
    recompute_pos,
):
    anywhere = pl.BlockSpec(memory_space=pl.ANY)
    vmem = pl.BlockSpec(memory_space=pltpu.VMEM)
    smem = pl.BlockSpec(memory_space=pltpu.SMEM)
    bf16 = jnp.bfloat16
    dma = pltpu.SemaphoreType.DMA
    return pl.pallas_call(
        kernel,
        out_shape=jax.ShapeDtypeStruct((REQ_DEV * RT, GROUP * HD), bf16),
        in_specs=[
            anywhere,
            vmem,
            anywhere,
            anywhere,
            anywhere,
            anywhere,
            vmem,
            smem,
            smem,
            smem,
            vmem,
        ],
        out_specs=vmem,
        scratch_shapes=[
            pltpu.VMEM((5, 4 * FEAT, WT), bf16),
            pltpu.VMEM((4, REQ_DEV * RT, FEAT), bf16),
            pltpu.VMEM((4, 2 * RT, FEAT), bf16),
            pltpu.VMEM((STORED, PT, 2 * HD), bf16),
            pltpu.VMEM((STORED, PT, 2 * HD), bf16),
            pltpu.VMEM((STORED, PT, 2 * HD), bf16),
            pltpu.VMEM((STORED, PT, 2 * HD), bf16),
            pltpu.VMEM((SIDE, SYS_DEV, 2 * HD), bf16),
            pltpu.VMEM((8, SLOTS, PT, 2 * HD), bf16),
            pltpu.VMEM((8, SLOTS, PT, 2 * HD), bf16),
            pltpu.VMEM((8, SIDE, SYS_DEV, 2 * HD), bf16),
            pltpu.VMEM((8, 128), jnp.int32),
            pltpu.SMEM((8, 128), jnp.int32),
            pltpu.VMEM((7, 8, 128), jnp.int32),
            pltpu.SMEM((7, 8, 128), jnp.int32),
            pltpu.SMEM((REQ_DEV * MAXP,), jnp.int32),
            pltpu.SMEM((REQ_DEV * MAXP,), jnp.int32),
            pltpu.VMEM((REQ_DEV, 10 * RT, HD), bf16),
            pltpu.VMEM((6, ROWS, HD), jnp.float32),
            pltpu.VMEM((6, ROWS, HD), jnp.float32),
            pltpu.VMEM((5, 2 * RT, WT), jnp.float32),
            pltpu.VMEM((8, 128), jnp.float32),
            pltpu.VMEM((3, 8, 128), jnp.float32),
            pltpu.VMEM((8 * RT, 1), jnp.float32),
            pltpu.VMEM((RT, MAXP * PT + 128), jnp.float32),
            dma((4, 8)),
            dma((4, 8)),
            dma((3,)),
            dma((3,)),
            dma((4,)),
            dma((4,)),
            dma((3,)),
            dma((3,)),
            dma((8,)),
            dma((8,)),
            dma((8, SIDE)),
            dma((8, SIDE)),
            dma((8,)),
            dma((8,)),
            dma((9,)),
        ],
        compiler_params=pltpu.CompilerParams(
            collective_id=0, has_side_effects=True, vmem_limit_bytes=64 * 1024 * 1024
        ),
    )(
        hidden,
        norm_gain.reshape(1, 4 * FEAT),
        w_query,
        w_key,
        w_value,
        passage_cache.reshape(STORED, PT, 2 * HD),
        sys_cache.reshape(SYS_DEV, 2 * HD),
        passage_place,
        passage_ids.T,
        passage_count,
        recompute_pos,
    )


def solution(mesh):
    placed = (
        P("req", "store"),
        P(),
        P(None, "store"),
        P(None, "store"),
        P(None, "store"),
        P("req", "store", None, None),
        P("req", "store", None),
        P(),
        P("req", None),
        P("req"),
        P("req", None),
    )
    return jax.shard_map(
        body, mesh=mesh, in_specs=placed, out_specs=P("req", "store"), check_vma=False
    )
```

```python
import jax
import jax.numpy as jnp
from jax import lax
from jax.experimental import pallas as pl
from jax.experimental.pallas import tpu as pltpu
from jax.sharding import PartitionSpec as P

HD = 128
GROUP = 8
PT = 256
MAXP = 4
RT = 80
SIDE = 4
FEAT = 2048
REQ_DEV = 8
STORED = 8
CAP = 2
SLOTS = SIDE * CAP
SYS = 1024
SYS_DEV = 32
WT = 256
ROWS = GROUP * RT
HALF = ROWS // 2
FAR = 1 << 20
LOW = -1e30
EXP_SCALE = HD ** (-0.5) * 1.4426950408889634
MESH = pl.DeviceIdType.MESH


def kernel(
    hidden,
    gain,
    w_query,
    w_key,
    w_value,
    stored,
    sys_own,
    place,
    ids,
    count,
    pos,
    out,
    weights,
    tokens,
    normed,
    along_own,
    along_one,
    along_two,
    along_three,
    along_sys,
    picked,
    held,
    held_sys,
    mine,
    mine_s,
    wishes,
    wishes_s,
    holder_s,
    spot,
    projected,
    part_mix,
    part_stat,
    partial,
    square_own,
    square_in,
    inverse,
    bias,
    z_send,
    z_recv,
    q_send,
    q_recv,
    a_send,
    a_recv,
    as_send,
    as_recv,
    w_send,
    w_recv,
    b_send,
    b_recv,
    bs_send,
    bs_recv,
    local,
):
    z = lax.axis_index("store")
    req = lax.axis_index("req")
    x = req // 8
    y = lax.rem(req // 2, 4)
    c = lax.rem(req, 2)
    a_pos = x * (1 - c) + y * c
    b_pos = y * (1 - c) + x * c

    def at(xx, yy, cc):
        return (z, (lax.rem(xx, 4) * 4 + lax.rem(yy, 4)) * 2 + cc)

    def along_dev(d):
        return at(x + d * (1 - c), y + d * c, c)

    def asker(db, dc):
        cc = c if dc == 0 else 1 - c
        return at(x + db * c, y + db * (1 - c), cc)

    def via(e, dc):
        cc = c if dc == 0 else 1 - c
        return at(x + e * cc, y + e * (1 - cc), cc)

    def via_index(e, dc):
        cc = c if dc == 0 else 1 - c
        return cc * 4 + lax.rem(y * (1 - cc) + x * cc + e, 4)

    right = (lax.rem(z + 1, 4), req)
    left = (lax.rem(z + 3, 4), req)
    me_via = c * 4 + b_pos
    along = (along_own, along_one, along_two, along_three)

    pieces = []
    for j in range(4):
        pieces.append((w_query.at[:, pl.ds(j * WT, WT)], weights.at[j]))
    pieces.append((w_key, weights.at[4, :, pl.ds(0, HD)]))
    pieces.append((w_value, weights.at[4, :, pl.ds(HD, HD)]))
    pieces.append((hidden, tokens.at[0]))
    pieces.append((stored, along_own))
    pieces.append((sys_own, along_sys.at[a_pos]))
    loads = [pltpu.make_async_copy(s, d, local.at[i]) for i, (s, d) in enumerate(pieces)]

    barrier = pltpu.get_barrier_semaphore()
    opposite = (lax.rem(z + 2, 4), req)
    partners = [left, right, opposite, at(x, y, 1 - c)]
    for d in range(1, 4):
        for cc in range(2):
            partners.append(at(x + d, y, cc))
            partners.append(at(x, y + d, cc))
    for device in partners:
        pl.semaphore_signal(barrier, inc=1, device_id=device, device_id_type=MESH)
    for load in loads[-3:]:
        load.start()
    pl.semaphore_wait(barrier, len(partners))

    def remote(src, dst, send, recv, device):
        return pltpu.make_async_remote_copy(
            src_ref=src,
            dst_ref=dst,
            send_sem=send,
            recv_sem=recv,
            device_id=device,
            device_id_type=MESH,
        )

    def rows_of(t):
        return pl.ds(pl.multiple_of(t * RT, 16), RT)

    def z_own(t, way):
        return remote(
            hidden.at[rows_of(t)],
            tokens.at[1 + way, rows_of(t)],
            z_send.at[way, t],
            z_recv.at[way, t],
            (right, left)[way],
        )

    def z_pass(t, way):
        cols = pl.ds(way * (FEAT // 2), FEAT // 2)
        return remote(
            tokens.at[1 + way, rows_of(t), cols],
            tokens.at[3, rows_of(t), cols],
            z_send.at[2 + way, t],
            z_recv.at[2 + way, t],
            (right, left)[way],
        )

    def a_copy(d):
        return remote(stored, along[d], a_send.at[d - 1], a_recv.at[d - 1], along_dev(d))

    def a_pass(d):
        part = pl.ds(0 if d == 1 else STORED // 2, STORED // 2)
        return remote(
            along[d].at[part], along_two.at[part], a_send.at[d], a_recv.at[d], along_dev(d)
        )

    def as_copy(d, at_pos):
        return remote(sys_own, along_sys.at[at_pos], as_send.at[d - 1], as_recv.at[d - 1], along_dev(d))

    def wish_copy(e, dc):
        slot = ((4 - e) % 4) * 2 + dc
        return remote(mine, wishes.at[slot - 1], w_send.at[slot], w_recv.at[slot], via(e, dc))

    def b_copy(db, dc, off, index):
        q = db * 2 + dc
        part = pl.ds(off * CAP, CAP)
        return remote(
            picked.at[q, part],
            held.at[index, part],
            b_send.at[q, off],
            b_recv.at[q, off],
            asker(db, dc),
        )

    def bs_copy(db, dc, index):
        q = db * 2 + dc
        return remote(along_sys, held_sys.at[index], bs_send.at[q], bs_recv.at[q], asker(db, dc))

    others = [(db, dc) for db in (1, 3, 2, 0) for dc in range(2) if (db, dc) != (0, 0)]

    for way in range(2):
        z_own(0, way).start()
    for d in (1, 3, 2):
        as_copy(d, a_pos).start()
    for d in (1, 3):
        a_copy(d).start()
    for way in range(2):
        z_own(1, way).start()

    cells = lax.broadcasted_iota(jnp.int32, (8, 128), 0) * 128 + lax.broadcasted_iota(
        jnp.int32, (8, 128), 1
    )

    def ask(i, wish):
        r = i // MAXP
        stands = place[ids[lax.rem(i, MAXP), r]]
        valid = lax.rem(i, MAXP) < count[r]
        holder = lax.div(stands, STORED)
        row = lax.rem(stands, STORED)
        hx, hy, hc = lax.div(holder, 8), lax.rem(lax.div(holder, 2), 4), lax.rem(holder, 2)
        rank = 0
        for j in range(REQ_DEV * MAXP):
            rank = rank + jnp.where(holder_s[j] == holder, 1, 0)
        rank = jnp.minimum(rank, CAP - 1)
        holder_s[i] = jnp.where(valid, holder, -1)
        through = hc * 4 + hy * (1 - hc) + hx * hc
        ahead = (hx - x + 4) * (1 - hc) + (hy - y + 4) * hc
        which = lax.rem(ahead, 4) * CAP + rank
        spot[i] = jnp.where(valid, through * SLOTS + which, spot[r * MAXP])
        cell = jnp.where(valid, through * 128 + which, -1)
        return jnp.where(cells == cell, row, wish)

    for i in range(REQ_DEV * MAXP):
        holder_s[i] = -1
        spot[i] = 0
    mine[...] = lax.fori_loop(0, REQ_DEV * MAXP, ask, jnp.zeros((8, 128), jnp.int32))
    for db, dc in others:
        wish_copy((4 - db) % 4, dc).start()

    eye = lax.broadcasted_iota(jnp.int32, (RT, RT), 0) == lax.broadcasted_iota(
        jnp.int32, (RT, RT), 1
    )

    def square_copy(d):
        device = (right, opposite, left)[d - 1]
        return remote(square_own, square_in.at[d - 1], q_send.at[d - 1], q_recv.at[d - 1], device)

    def square(t, _):
        column = jnp.zeros((RT, 1), jnp.float32)
        for part in range(FEAT // 256):
            wide = tokens[0, rows_of(t), pl.ds(part * 256, 256)].astype(jnp.float32)
            column = column + jnp.sum(wide * wide, axis=1, keepdims=True)
        square_own[pl.ds(t, 1), pl.ds(0, RT)] = jnp.sum(
            jnp.where(eye, column, 0.0), axis=0, keepdims=True
        )
        return 0

    square_own[...] = jnp.zeros((8, 128), jnp.float32)
    loads[-3].wait()
    lax.fori_loop(0, 8, square, 0)
    for d in (1, 3, 2):
        square_copy(d).start()

    def invert(t, _):
        line = square_own[pl.ds(t, 1), pl.ds(0, RT)]
        for d in range(3):
            line = line + square_in[d, pl.ds(t, 1), pl.ds(0, RT)]
        line = lax.rsqrt(line * (1.0 / (4 * FEAT)) + 1e-05)
        inverse[rows_of(t), :] = jnp.sum(
            jnp.where(eye, jnp.broadcast_to(line, (RT, RT)), 0.0), axis=1, keepdims=True
        )
        return 0

    def mark(r):
        line = pos[pl.ds(r, 1), :]
        wide = jnp.broadcast_to(line, (RT, RT))
        column = jnp.sum(jnp.where(eye, wide, 0), axis=1, keepdims=True)
        limit = jnp.minimum(column, count[r] * PT - 1)
        offsets = lax.broadcasted_iota(jnp.int32, (RT, MAXP * PT), 1)
        touched = jnp.max(jnp.where(offsets == column, FAR, 0), axis=0, keepdims=True)
        stored_code = jnp.maximum(jnp.broadcast_to(touched, offsets.shape), offsets)
        bias[:, pl.ds(0, MAXP * PT)] = jnp.where(stored_code <= limit, 0.0, LOW)
        bias[:, pl.ds(MAXP * PT, RT)] = jnp.where(wide <= limit, 0.0, LOW)

    def give(off):
        rows = along[(4 - off) % 4]
        for db, dc in others + [(0, 0)]:
            q = db * 2 + dc
            for rank in range(CAP):
                k = off * CAP + rank
                row = wishes_s[q - 1, me_via, k] if q else mine_s[me_via, k]
                if q:
                    picked[q, k] = rows[row]
                else:
                    held[me_via, k] = rows[row]
            if q:
                b_copy(db, dc, off, me_via).start()

    def give_own():
        for load in loads[-2:]:
            load.wait()
        for d in (1, 3, 2):
            as_copy(d, lax.rem(a_pos + 4 - d, 4)).wait_recv()
        for db, dc in others:
            bs_copy(db, dc, me_via).start()
        held_sys[me_via] = along_sys[...]
        for db, dc in others:
            wish_copy((4 - db) % 4, dc).wait_recv()
        for source, target in ((wishes, wishes_s), (mine, mine_s)):
            copy = pltpu.make_async_copy(source, target, local.at[0])
            copy.start()
            copy.wait()
        give(0)

    def give_near():
        for d in (1, 3):
            a_copy(d).wait_recv()
            a_pass(d).start()
        give(3)
        give(1)

    def give_far():
        for d in (1, 3):
            a_pass(d).wait_recv()
        give(2)

    spread = (0, 3, 1, 2)

    def scale(k, slots):
        def norm(i, _):
            rows = pl.ds(pl.multiple_of(k * (2 * RT) + i * 16, 16), 16)
            to = pl.ds(pl.multiple_of(i * 16, 16), 16)
            for slot in slots:
                source = lax.rem(z + spread[slot], 4)
                cols = pl.ds(pl.multiple_of(source * FEAT, FEAT), FEAT)
                wide = tokens[slot, rows, :].astype(jnp.float32)
                normed[slot, to, :] = (wide * inverse[rows, :] * gain[:, cols]).astype(jnp.bfloat16)
            return 0

        lax.fori_loop(0, 2 * RT // 16, norm, 0)

    def product(j, slot):
        source = lax.rem(z + spread[slot], 4)
        rows = pl.ds(pl.multiple_of(source * FEAT, FEAT), FEAT)
        return jnp.dot(normed[slot], weights[j, rows, :], preferred_element_type=jnp.float32)

    def project_near(k):
        scale(k, (0, 1, 2))

        def tile(j, _):
            partial[j] = product(j, 0) + product(j, 1) + product(j, 2)
            return 0

        lax.fori_loop(0, 5, tile, 0)

    def project_far(k):
        for step in range(2):
            for way in range(2):
                z_pass(2 * k + step, way).wait_recv()
        scale(k, (3,))

        def tile(j, _):
            low = (partial[j] + product(j, 3)).astype(jnp.bfloat16)
            for half in range(2):
                for step in range(2):
                    to = pl.ds(pl.multiple_of((2 * j + half) * RT, 16), RT)
                    projected[2 * k + step, to, :] = low[
                        step * RT : (step + 1) * RT, half * HD : (half + 1) * HD
                    ]
            return 0

        lax.fori_loop(0, 5, tile, 0)

    def dot_t(a, b):
        return lax.dot_general(a, b, (((1,), (1,)), ((), ())), preferred_element_type=jnp.float32)

    def half_rows(hb):
        return pl.ds(hb * HALF, HALF)

    def shared(r, _):
        for hb in range(2):
            shared_half(r, hb)
        return 0

    def shared_half(r, hb):
        rows = half_rows(hb)
        query = projected[r, rows, :]
        keyvals = held_sys[...].reshape(SYS, 2 * HD)
        scores = dot_t(query, keyvals[:, :HD])
        largest = jnp.max(scores, axis=1, keepdims=True)
        part = jnp.exp2((scores - largest) * EXP_SCALE)
        total = jnp.sum(part, axis=1, keepdims=True)
        mix = jnp.dot(
            part.astype(jnp.bfloat16), keyvals[:, HD:], preferred_element_type=jnp.float32
        )
        slot = lax.rem(r, 6)
        part_mix[slot, rows, :] = mix
        lane = lax.broadcasted_iota(jnp.int32, (HALF, HD), 1)
        part_stat[slot, rows, :] = jnp.where(lane < HD // 2, largest, total)

    def own(r, _):
        mark(r)
        for hb in range(2):
            own_half(r, hb)
        return 0

    def own_half(r, hb):
        rows = half_rows(hb)
        slot = lax.rem(r, 6)
        query = projected[r, rows, :]

        def masked(one, first, width):
            hide = bias[:, pl.ds(first, width)]
            return one + jnp.concatenate([hide] * (GROUP // 2), axis=0)

        spots = [spot[r * MAXP + j] for j in range(MAXP)]
        scores = []
        for j in range(MAXP):
            keys = held[spots[j] // SLOTS, lax.rem(spots[j], SLOTS), :, pl.ds(0, HD)]
            scores.append(masked(dot_t(query, keys), j * PT, PT))
        keys = projected[r, pl.ds(ROWS, RT), :]
        scores.append(masked(dot_t(query, keys), MAXP * PT, RT))
        stat = part_stat[slot, rows, :]
        sys_largest = stat[:, 0:1]
        sys_total = stat[:, HD // 2 : HD // 2 + 1]
        largest = sys_largest
        for one in scores:
            largest = jnp.maximum(largest, jnp.max(one, axis=1, keepdims=True))
        shrink = jnp.exp2((sys_largest - largest) * EXP_SCALE)
        total = sys_total * shrink
        mix = part_mix[slot, rows, :] * shrink
        for j in range(MAXP + 1):
            part = jnp.exp2((scores[j] - largest) * EXP_SCALE)
            total = total + jnp.sum(part, axis=1, keepdims=True)
            if j < MAXP:
                values = held[spots[j] // SLOTS, lax.rem(spots[j], SLOTS), :, pl.ds(HD, HD)]
            else:
                values = projected[r, pl.ds(ROWS + RT, RT), :]
            mix = mix + jnp.dot(
                part.astype(jnp.bfloat16), values, preferred_element_type=jnp.float32
            )
        result = (mix / total).astype(jnp.bfloat16)
        to = pl.ds(pl.multiple_of(r * RT, 16), RT)
        for h in range(GROUP // 2):
            cols = pl.ds((hb * (GROUP // 2) + h) * HD, HD)
            out[to, cols] = result[h * RT : (h + 1) * RT, :]

    def step(t, _):
        @pl.when(t < 8)
        def _():
            for way in range(2):
                z_own(t, way).wait_recv()
                z_pass(t, way).start()

            @pl.when(t < 6)
            def _():
                for way in range(2):
                    z_own(t + 2, way).start()

        @pl.when(t == 0)
        def _():
            give_own()
            loads[0].start()
            loads[1].start()

        @pl.when(t == 1)
        def _():
            give_near()
            for load in loads[2:4]:
                load.start()

        @pl.when(t == 2)
        def _():
            give_far()
            for load in loads[4:-3]:
                load.start()
            for d in (1, 3, 2):
                square_copy(d).wait_recv()
            lax.fori_loop(0, 8, invert, 0)
            for load in loads[:-3]:
                load.wait()

        @pl.when(t == 3)
        def _():
            for db, dc in others:
                bs_copy(db, dc, via_index((4 - db) % 4, dc)).wait_recv()

        @pl.when(t == 6)
        def _():
            for db, dc in others:
                for off in range(SIDE):
                    b_copy(db, dc, off, via_index((4 - db) % 4, dc)).wait_recv()

        @pl.when(t >= 6)
        def _():
            begin = jnp.where(t == 6, 0, jnp.where(t == 7, 2, 6))
            end = jnp.where(t == 6, 2, jnp.where(t == 9, 8, 6))
            lax.fori_loop(begin, end, own, 0)

        @pl.when((t == 3) | (t == 5) | (t == 6) | (t == 8))
        def _():
            k = (t - 2) // 2
            project_far(k)
            lax.fori_loop(2 * k, 2 * k + 2, shared, 0)

        @pl.when((t == 2) | (t == 4) | (t == 5) | (t == 7))
        def _():
            project_near((t - 1) // 2)

        return 0

    lax.fori_loop(0, 10, step, 0)

    def finish(t, _):
        for way in range(2):
            z_own(t, way).wait_send()
            z_pass(t, way).wait_send()
        return 0

    lax.fori_loop(0, 8, finish, 0)
    for d in (1, 3, 2):
        square_copy(d).wait_send()
    for d in (1, 3):
        a_copy(d).wait_send()
        a_pass(d).wait_send()
    for d in (1, 3, 2):
        as_copy(d, a_pos).wait_send()
    for db, dc in others:
        wish_copy((4 - db) % 4, dc).wait_send()
        for off in range(SIDE):
            b_copy(db, dc, off, me_via).wait_send()
        bs_copy(db, dc, me_via).wait_send()


def body(
    hidden,
    norm_gain,
    w_query,
    w_key,
    w_value,
    passage_cache,
    sys_cache,
    passage_place,
    passage_ids,
    passage_count,
    recompute_pos,
):
    anywhere = pl.BlockSpec(memory_space=pl.ANY)
    vmem = pl.BlockSpec(memory_space=pltpu.VMEM)
    smem = pl.BlockSpec(memory_space=pltpu.SMEM)
    bf16 = jnp.bfloat16
    dma = pltpu.SemaphoreType.DMA
    return pl.pallas_call(
        kernel,
        out_shape=jax.ShapeDtypeStruct((REQ_DEV * RT, GROUP * HD), bf16),
        in_specs=[
            anywhere,
            vmem,
            anywhere,
            anywhere,
            anywhere,
            anywhere,
            vmem,
            smem,
            smem,
            smem,
            vmem,
        ],
        out_specs=vmem,
        scratch_shapes=[
            pltpu.VMEM((5, 4 * FEAT, WT), bf16),
            pltpu.VMEM((4, REQ_DEV * RT, FEAT), bf16),
            pltpu.VMEM((4, 2 * RT, FEAT), bf16),
            pltpu.VMEM((STORED, PT, 2 * HD), bf16),
            pltpu.VMEM((STORED, PT, 2 * HD), bf16),
            pltpu.VMEM((STORED, PT, 2 * HD), bf16),
            pltpu.VMEM((STORED, PT, 2 * HD), bf16),
            pltpu.VMEM((SIDE, SYS_DEV, 2 * HD), bf16),
            pltpu.VMEM((8, SLOTS, PT, 2 * HD), bf16),
            pltpu.VMEM((8, SLOTS, PT, 2 * HD), bf16),
            pltpu.VMEM((8, SIDE, SYS_DEV, 2 * HD), bf16),
            pltpu.VMEM((8, 128), jnp.int32),
            pltpu.SMEM((8, 128), jnp.int32),
            pltpu.VMEM((7, 8, 128), jnp.int32),
            pltpu.SMEM((7, 8, 128), jnp.int32),
            pltpu.SMEM((REQ_DEV * MAXP,), jnp.int32),
            pltpu.SMEM((REQ_DEV * MAXP,), jnp.int32),
            pltpu.VMEM((REQ_DEV, 10 * RT, HD), bf16),
            pltpu.VMEM((6, ROWS, HD), jnp.float32),
            pltpu.VMEM((6, ROWS, HD), jnp.float32),
            pltpu.VMEM((5, 2 * RT, WT), jnp.float32),
            pltpu.VMEM((8, 128), jnp.float32),
            pltpu.VMEM((3, 8, 128), jnp.float32),
            pltpu.VMEM((8 * RT, 1), jnp.float32),
            pltpu.VMEM((RT, MAXP * PT + 128), jnp.float32),
            dma((4, 8)),
            dma((4, 8)),
            dma((3,)),
            dma((3,)),
            dma((4,)),
            dma((4,)),
            dma((3,)),
            dma((3,)),
            dma((8,)),
            dma((8,)),
            dma((8, SIDE)),
            dma((8, SIDE)),
            dma((8,)),
            dma((8,)),
            dma((9,)),
        ],
        compiler_params=pltpu.CompilerParams(
            collective_id=0, has_side_effects=True, vmem_limit_bytes=64 * 1024 * 1024
        ),
    )(
        hidden,
        norm_gain.reshape(1, 4 * FEAT),
        w_query,
        w_key,
        w_value,
        passage_cache.reshape(STORED, PT, 2 * HD),
        sys_cache.reshape(SYS_DEV, 2 * HD),
        passage_place,
        passage_ids.T,
        passage_count,
        recompute_pos,
    )


def solution(mesh):
    placed = (
        P("req", "store"),
        P(),
        P(None, "store"),
        P(None, "store"),
        P(None, "store"),
        P("req", "store", None, None),
        P("req", "store", None),
        P(),
        P("req", None),
        P("req"),
        P("req", None),
    )
    return jax.shard_map(
        body, mesh=mesh, in_specs=placed, out_specs=P("req", "store"), check_vma=False
    )
```

```python
import jax
import jax.numpy as jnp
from jax import lax
from jax.experimental import pallas as pl
from jax.experimental.pallas import tpu as pltpu
from jax.sharding import PartitionSpec as P

HD = 128
GROUP = 8
PT = 256
MAXP = 4
RT = 80
SIDE = 4
FEAT = 2048
REQ_DEV = 8
STORED = 8
CAP = 2
SLOTS = SIDE * CAP
SYS = 1024
SYS_DEV = 32
WT = 256
ROWS = GROUP * RT
HALF = ROWS // 2
FAR = 1 << 20
LOW = -1e30
EXP_SCALE = HD ** (-0.5) * 1.4426950408889634
MESH = pl.DeviceIdType.MESH


def kernel(
    hidden,
    gain,
    w_query,
    w_key,
    w_value,
    stored,
    sys_own,
    place,
    ids,
    count,
    pos,
    out,
    weights,
    tokens,
    normed,
    along_own,
    along_one,
    along_two,
    along_three,
    along_sys,
    picked,
    held,
    held_sys,
    mine,
    mine_s,
    wishes,
    wishes_s,
    holder_s,
    spot,
    projected,
    part_mix,
    part_stat,
    partial,
    square_own,
    square_in,
    inverse,
    bias,
    z_send,
    z_recv,
    q_send,
    q_recv,
    a_send,
    a_recv,
    as_send,
    as_recv,
    w_send,
    w_recv,
    b_send,
    b_recv,
    bs_send,
    bs_recv,
    local,
):
    z = lax.axis_index("store")
    req = lax.axis_index("req")
    x = req // 8
    y = lax.rem(req // 2, 4)
    c = lax.rem(req, 2)
    a_pos = x * (1 - c) + y * c
    b_pos = y * (1 - c) + x * c

    def at(xx, yy, cc):
        return (z, (lax.rem(xx, 4) * 4 + lax.rem(yy, 4)) * 2 + cc)

    def along_dev(d):
        return at(x + d * (1 - c), y + d * c, c)

    def asker(db, dc):
        cc = c if dc == 0 else 1 - c
        return at(x + db * c, y + db * (1 - c), cc)

    def via(e, dc):
        cc = c if dc == 0 else 1 - c
        return at(x + e * cc, y + e * (1 - cc), cc)

    def via_index(e, dc):
        cc = c if dc == 0 else 1 - c
        return cc * 4 + lax.rem(y * (1 - cc) + x * cc + e, 4)

    right = (lax.rem(z + 1, 4), req)
    left = (lax.rem(z + 3, 4), req)
    me_via = c * 4 + b_pos
    along = (along_own, along_one, along_two, along_three)

    pieces = []
    for j in range(4):
        pieces.append((w_query.at[:, pl.ds(j * WT, WT)], weights.at[j]))
    pieces.append((w_key, weights.at[4, :, pl.ds(0, HD)]))
    pieces.append((w_value, weights.at[4, :, pl.ds(HD, HD)]))
    pieces.append((hidden, tokens.at[0]))
    pieces.append((stored, along_own))
    pieces.append((sys_own, along_sys.at[a_pos]))
    loads = [pltpu.make_async_copy(s, d, local.at[i]) for i, (s, d) in enumerate(pieces)]

    barrier = pltpu.get_barrier_semaphore()
    opposite = (lax.rem(z + 2, 4), req)
    partners = [left, right, opposite, at(x, y, 1 - c)]
    for d in range(1, 4):
        for cc in range(2):
            partners.append(at(x + d, y, cc))
            partners.append(at(x, y + d, cc))
    for device in partners:
        pl.semaphore_signal(barrier, inc=1, device_id=device, device_id_type=MESH)
    for load in loads[-3:]:
        load.start()
    pl.semaphore_wait(barrier, len(partners))

    def remote(src, dst, send, recv, device):
        return pltpu.make_async_remote_copy(
            src_ref=src,
            dst_ref=dst,
            send_sem=send,
            recv_sem=recv,
            device_id=device,
            device_id_type=MESH,
        )

    def rows_of(t):
        return pl.ds(pl.multiple_of(t * RT, 16), RT)

    def z_own(t, way):
        return remote(
            hidden.at[rows_of(t)],
            tokens.at[1 + way, rows_of(t)],
            z_send.at[way, t],
            z_recv.at[way, t],
            (right, left)[way],
        )

    def z_pass(t, way):
        cols = pl.ds(way * (FEAT // 2), FEAT // 2)
        return remote(
            tokens.at[1 + way, rows_of(t), cols],
            tokens.at[3, rows_of(t), cols],
            z_send.at[2 + way, t],
            z_recv.at[2 + way, t],
            (right, left)[way],
        )

    def a_copy(d):
        return remote(stored, along[d], a_send.at[d - 1], a_recv.at[d - 1], along_dev(d))

    def a_pass(d):
        part = pl.ds(0 if d == 1 else STORED // 2, STORED // 2)
        return remote(
            along[d].at[part], along_two.at[part], a_send.at[d], a_recv.at[d], along_dev(d)
        )

    def as_copy(d, at_pos):
        return remote(sys_own, along_sys.at[at_pos], as_send.at[d - 1], as_recv.at[d - 1], along_dev(d))

    def wish_copy(e, dc):
        slot = ((4 - e) % 4) * 2 + dc
        return remote(mine, wishes.at[slot - 1], w_send.at[slot], w_recv.at[slot], via(e, dc))

    def b_copy(db, dc, off, index):
        q = db * 2 + dc
        part = pl.ds(off * CAP, CAP)
        return remote(
            picked.at[q, part],
            held.at[index, part],
            b_send.at[q, off],
            b_recv.at[q, off],
            asker(db, dc),
        )

    def bs_copy(db, dc, index):
        q = db * 2 + dc
        return remote(along_sys, held_sys.at[index], bs_send.at[q], bs_recv.at[q], asker(db, dc))

    others = [(db, dc) for db in (1, 3, 2, 0) for dc in range(2) if (db, dc) != (0, 0)]

    for way in range(2):
        z_own(0, way).start()
    for d in (1, 3, 2):
        as_copy(d, a_pos).start()
    for d in (1, 3):
        a_copy(d).start()
    for way in range(2):
        z_own(1, way).start()

    cells = lax.broadcasted_iota(jnp.int32, (8, 128), 0) * 128 + lax.broadcasted_iota(
        jnp.int32, (8, 128), 1
    )

    def ask(i, wish):
        r = i // MAXP
        stands = place[ids[lax.rem(i, MAXP), r]]
        valid = lax.rem(i, MAXP) < count[r]
        holder = lax.div(stands, STORED)
        row = lax.rem(stands, STORED)
        hx, hy, hc = lax.div(holder, 8), lax.rem(lax.div(holder, 2), 4), lax.rem(holder, 2)
        rank = 0
        for j in range(REQ_DEV * MAXP):
            rank = rank + jnp.where(holder_s[j] == holder, 1, 0)
        rank = jnp.minimum(rank, CAP - 1)
        holder_s[i] = jnp.where(valid, holder, -1)
        through = hc * 4 + hy * (1 - hc) + hx * hc
        ahead = (hx - x + 4) * (1 - hc) + (hy - y + 4) * hc
        which = lax.rem(ahead, 4) * CAP + rank
        spot[i] = jnp.where(valid, through * SLOTS + which, spot[r * MAXP])
        cell = jnp.where(valid, through * 128 + which, -1)
        return jnp.where(cells == cell, row, wish)

    for i in range(REQ_DEV * MAXP):
        holder_s[i] = -1
        spot[i] = 0
    mine[...] = lax.fori_loop(0, REQ_DEV * MAXP, ask, jnp.zeros((8, 128), jnp.int32))
    for db, dc in others:
        wish_copy((4 - db) % 4, dc).start()

    eye = lax.broadcasted_iota(jnp.int32, (RT, RT), 0) == lax.broadcasted_iota(
        jnp.int32, (RT, RT), 1
    )

    def square_copy(d):
        device = (right, opposite, left)[d - 1]
        return remote(square_own, square_in.at[d - 1], q_send.at[d - 1], q_recv.at[d - 1], device)

    def square(t, _):
        column = jnp.zeros((RT, 1), jnp.float32)
        for part in range(FEAT // 256):
            wide = tokens[0, rows_of(t), pl.ds(part * 256, 256)].astype(jnp.float32)
            column = column + jnp.sum(wide * wide, axis=1, keepdims=True)
        square_own[pl.ds(t, 1), pl.ds(0, RT)] = jnp.sum(
            jnp.where(eye, column, 0.0), axis=0, keepdims=True
        )
        return 0

    square_own[...] = jnp.zeros((8, 128), jnp.float32)
    loads[-3].wait()
    lax.fori_loop(0, 8, square, 0)
    for d in (1, 3, 2):
        square_copy(d).start()

    def invert(t, _):
        line = square_own[pl.ds(t, 1), pl.ds(0, RT)]
        for d in range(3):
            line = line + square_in[d, pl.ds(t, 1), pl.ds(0, RT)]
        line = lax.rsqrt(line * (1.0 / (4 * FEAT)) + 1e-05)
        inverse[rows_of(t), :] = jnp.sum(
            jnp.where(eye, jnp.broadcast_to(line, (RT, RT)), 0.0), axis=1, keepdims=True
        )
        return 0

    def mark(r):
        line = pos[pl.ds(r, 1), :]
        wide = jnp.broadcast_to(line, (RT, RT))
        column = jnp.sum(jnp.where(eye, wide, 0), axis=1, keepdims=True)
        limit = jnp.minimum(column, count[r] * PT - 1)
        offsets = lax.broadcasted_iota(jnp.int32, (RT, MAXP * PT), 1)
        touched = jnp.max(jnp.where(offsets == column, FAR, 0), axis=0, keepdims=True)
        stored_code = jnp.maximum(jnp.broadcast_to(touched, offsets.shape), offsets)
        bias[:, pl.ds(0, MAXP * PT)] = jnp.where(stored_code <= limit, 0.0, LOW)
        bias[:, pl.ds(MAXP * PT, RT)] = jnp.where(wide <= limit, 0.0, LOW)

    def give(off):
        rows = along[(4 - off) % 4]
        for db, dc in others + [(0, 0)]:
            q = db * 2 + dc
            for rank in range(CAP):
                k = off * CAP + rank
                row = wishes_s[q - 1, me_via, k] if q else mine_s[me_via, k]
                if q:
                    picked[q, k] = rows[row]
                else:
                    held[me_via, k] = rows[row]
            if q:
                b_copy(db, dc, off, me_via).start()

    def give_own():
        for load in loads[-2:]:
            load.wait()
        for d in (1, 3, 2):
            as_copy(d, lax.rem(a_pos + 4 - d, 4)).wait_recv()
        for db, dc in others:
            bs_copy(db, dc, me_via).start()
        held_sys[me_via] = along_sys[...]
        for db, dc in others:
            wish_copy((4 - db) % 4, dc).wait_recv()
        for source, target in ((wishes, wishes_s), (mine, mine_s)):
            copy = pltpu.make_async_copy(source, target, local.at[0])
            copy.start()
            copy.wait()
        give(0)

    def give_near():
        for d in (1, 3):
            a_copy(d).wait_recv()
            a_pass(d).start()
        give(3)
        give(1)

    def give_far():
        for d in (1, 3):
            a_pass(d).wait_recv()
        give(2)

    spread = (0, 3, 1, 2)

    def scale(k, slots):
        def norm(i, _):
            rows = pl.ds(pl.multiple_of(k * (2 * RT) + i * 16, 16), 16)
            to = pl.ds(pl.multiple_of(i * 16, 16), 16)
            for slot in slots:
                source = lax.rem(z + spread[slot], 4)
                cols = pl.ds(pl.multiple_of(source * FEAT, FEAT), FEAT)
                wide = tokens[slot, rows, :].astype(jnp.float32)
                normed[slot, to, :] = (wide * inverse[rows, :] * gain[:, cols]).astype(jnp.bfloat16)
            return 0

        lax.fori_loop(0, 2 * RT // 16, norm, 0)

    def product(j, slot):
        source = lax.rem(z + spread[slot], 4)
        rows = pl.ds(pl.multiple_of(source * FEAT, FEAT), FEAT)
        return jnp.dot(normed[slot], weights[j, rows, :], preferred_element_type=jnp.float32)

    def project_near(k):
        scale(k, (0, 1, 2))

        def tile(j, _):
            partial[j] = product(j, 0) + product(j, 1) + product(j, 2)
            return 0

        lax.fori_loop(0, 5, tile, 0)

    def project_far(k):
        for step in range(2):
            for way in range(2):
                z_pass(2 * k + step, way).wait_recv()
        scale(k, (3,))

        def tile(j, _):
            low = (partial[j] + product(j, 3)).astype(jnp.bfloat16)
            for half in range(2):
                for step in range(2):
                    to = pl.ds(pl.multiple_of((2 * j + half) * RT, 16), RT)
                    projected[2 * k + step, to, :] = low[
                        step * RT : (step + 1) * RT, half * HD : (half + 1) * HD
                    ]
            return 0

        lax.fori_loop(0, 5, tile, 0)

    def dot_t(a, b):
        return lax.dot_general(a, b, (((1,), (1,)), ((), ())), preferred_element_type=jnp.float32)

    def half_rows(hb):
        return pl.ds(hb * HALF, HALF)

    def shared(r, _):
        for hb in range(2):
            shared_half(r, hb)
        return 0

    def shared_half(r, hb):
        rows = half_rows(hb)
        query = projected[r, rows, :]
        keyvals = held_sys[...].reshape(SYS, 2 * HD)
        scores = dot_t(query, keyvals[:, :HD])
        largest = jnp.max(scores, axis=1, keepdims=True)
        part = jnp.exp2((scores - largest) * EXP_SCALE)
        total = jnp.sum(part, axis=1, keepdims=True)
        mix = jnp.dot(
            part.astype(jnp.bfloat16), keyvals[:, HD:], preferred_element_type=jnp.float32
        )
        slot = lax.rem(r, 6)
        part_mix[slot, rows, :] = mix
        lane = lax.broadcasted_iota(jnp.int32, (HALF, HD), 1)
        part_stat[slot, rows, :] = jnp.where(lane < HD // 2, largest, total)

    def own(r, _):
        mark(r)
        for hb in range(2):
            own_half(r, hb)
        return 0

    def own_half(r, hb):
        rows = half_rows(hb)
        slot = lax.rem(r, 6)
        query = projected[r, rows, :]

        def masked(one, first, width):
            hide = bias[:, pl.ds(first, width)]
            return one + jnp.concatenate([hide] * (GROUP // 2), axis=0)

        spots = [spot[r * MAXP + j] for j in range(MAXP)]
        scores = []
        for j in range(MAXP):
            keys = held[spots[j] // SLOTS, lax.rem(spots[j], SLOTS), :, pl.ds(0, HD)]
            scores.append(masked(dot_t(query, keys), j * PT, PT))
        keys = projected[r, pl.ds(ROWS, RT), :]
        scores.append(masked(dot_t(query, keys), MAXP * PT, RT))
        stat = part_stat[slot, rows, :]
        sys_largest = stat[:, 0:1]
        sys_total = stat[:, HD // 2 : HD // 2 + 1]
        largest = sys_largest
        for one in scores:
            largest = jnp.maximum(largest, jnp.max(one, axis=1, keepdims=True))
        shrink = jnp.exp2((sys_largest - largest) * EXP_SCALE)
        total = sys_total * shrink
        mix = part_mix[slot, rows, :] * shrink
        for j in range(MAXP + 1):
            part = jnp.exp2((scores[j] - largest) * EXP_SCALE)
            total = total + jnp.sum(part, axis=1, keepdims=True)
            if j < MAXP:
                values = held[spots[j] // SLOTS, lax.rem(spots[j], SLOTS), :, pl.ds(HD, HD)]
            else:
                values = projected[r, pl.ds(ROWS + RT, RT), :]
            mix = mix + jnp.dot(
                part.astype(jnp.bfloat16), values, preferred_element_type=jnp.float32
            )
        result = (mix / total).astype(jnp.bfloat16)
        to = pl.ds(pl.multiple_of(r * RT, 16), RT)
        for h in range(GROUP // 2):
            cols = pl.ds((hb * (GROUP // 2) + h) * HD, HD)
            out[to, cols] = result[h * RT : (h + 1) * RT, :]

    def step(t, _):
        @pl.when(t < 8)
        def _():
            for way in range(2):
                z_own(t, way).wait_recv()
                z_pass(t, way).start()

            @pl.when(t < 6)
            def _():
                for way in range(2):
                    z_own(t + 2, way).start()

        @pl.when(t == 0)
        def _():
            give_own()
            loads[0].start()
            loads[1].start()

        @pl.when(t == 1)
        def _():
            give_near()
            for load in loads[2:4]:
                load.start()

        @pl.when(t == 2)
        def _():
            give_far()
            for load in loads[4:-3]:
                load.start()
            for d in (1, 3, 2):
                square_copy(d).wait_recv()
            lax.fori_loop(0, 8, invert, 0)
            for load in loads[:-3]:
                load.wait()

        @pl.when(t == 3)
        def _():
            for db, dc in others:
                bs_copy(db, dc, via_index((4 - db) % 4, dc)).wait_recv()

        @pl.when(t == 6)
        def _():
            for db, dc in others:
                for off in range(SIDE):
                    b_copy(db, dc, off, via_index((4 - db) % 4, dc)).wait_recv()

        @pl.when(t >= 6)
        def _():
            begin = jnp.where(t == 6, 0, jnp.where(t == 7, 3, 6))
            end = jnp.where(t == 6, 3, jnp.where(t == 9, 8, 6))
            lax.fori_loop(begin, end, own, 0)

        @pl.when((t == 3) | (t == 5) | (t == 6) | (t == 8))
        def _():
            k = (t - 2) // 2
            project_far(k)
            lax.fori_loop(2 * k, 2 * k + 2, shared, 0)

        @pl.when((t == 2) | (t == 4) | (t == 5) | (t == 7))
        def _():
            project_near((t - 1) // 2)

        return 0

    lax.fori_loop(0, 10, step, 0)

    def finish(t, _):
        for way in range(2):
            z_own(t, way).wait_send()
            z_pass(t, way).wait_send()
        return 0

    lax.fori_loop(0, 8, finish, 0)
    for d in (1, 3, 2):
        square_copy(d).wait_send()
    for d in (1, 3):
        a_copy(d).wait_send()
        a_pass(d).wait_send()
    for d in (1, 3, 2):
        as_copy(d, a_pos).wait_send()
    for db, dc in others:
        wish_copy((4 - db) % 4, dc).wait_send()
        for off in range(SIDE):
            b_copy(db, dc, off, me_via).wait_send()
        bs_copy(db, dc, me_via).wait_send()


def body(
    hidden,
    norm_gain,
    w_query,
    w_key,
    w_value,
    passage_cache,
    sys_cache,
    passage_place,
    passage_ids,
    passage_count,
    recompute_pos,
):
    anywhere = pl.BlockSpec(memory_space=pl.ANY)
    vmem = pl.BlockSpec(memory_space=pltpu.VMEM)
    smem = pl.BlockSpec(memory_space=pltpu.SMEM)
    bf16 = jnp.bfloat16
    dma = pltpu.SemaphoreType.DMA
    return pl.pallas_call(
        kernel,
        out_shape=jax.ShapeDtypeStruct((REQ_DEV * RT, GROUP * HD), bf16),
        in_specs=[
            anywhere,
            vmem,
            anywhere,
            anywhere,
            anywhere,
            anywhere,
            vmem,
            smem,
            smem,
            smem,
            vmem,
        ],
        out_specs=vmem,
        scratch_shapes=[
            pltpu.VMEM((5, 4 * FEAT, WT), bf16),
            pltpu.VMEM((4, REQ_DEV * RT, FEAT), bf16),
            pltpu.VMEM((4, 2 * RT, FEAT), bf16),
            pltpu.VMEM((STORED, PT, 2 * HD), bf16),
            pltpu.VMEM((STORED, PT, 2 * HD), bf16),
            pltpu.VMEM((STORED, PT, 2 * HD), bf16),
            pltpu.VMEM((STORED, PT, 2 * HD), bf16),
            pltpu.VMEM((SIDE, SYS_DEV, 2 * HD), bf16),
            pltpu.VMEM((8, SLOTS, PT, 2 * HD), bf16),
            pltpu.VMEM((8, SLOTS, PT, 2 * HD), bf16),
            pltpu.VMEM((8, SIDE, SYS_DEV, 2 * HD), bf16),
            pltpu.VMEM((8, 128), jnp.int32),
            pltpu.SMEM((8, 128), jnp.int32),
            pltpu.VMEM((7, 8, 128), jnp.int32),
            pltpu.SMEM((7, 8, 128), jnp.int32),
            pltpu.SMEM((REQ_DEV * MAXP,), jnp.int32),
            pltpu.SMEM((REQ_DEV * MAXP,), jnp.int32),
            pltpu.VMEM((REQ_DEV, 10 * RT, HD), bf16),
            pltpu.VMEM((6, ROWS, HD), jnp.float32),
            pltpu.VMEM((6, ROWS, HD), jnp.float32),
            pltpu.VMEM((5, 2 * RT, WT), jnp.float32),
            pltpu.VMEM((8, 128), jnp.float32),
            pltpu.VMEM((3, 8, 128), jnp.float32),
            pltpu.VMEM((8 * RT, 1), jnp.float32),
            pltpu.VMEM((RT, MAXP * PT + 128), jnp.float32),
            dma((4, 8)),
            dma((4, 8)),
            dma((3,)),
            dma((3,)),
            dma((4,)),
            dma((4,)),
            dma((3,)),
            dma((3,)),
            dma((8,)),
            dma((8,)),
            dma((8, SIDE)),
            dma((8, SIDE)),
            dma((8,)),
            dma((8,)),
            dma((9,)),
        ],
        compiler_params=pltpu.CompilerParams(
            collective_id=0, has_side_effects=True, vmem_limit_bytes=64 * 1024 * 1024
        ),
    )(
        hidden,
        norm_gain.reshape(1, 4 * FEAT),
        w_query,
        w_key,
        w_value,
        passage_cache.reshape(STORED, PT, 2 * HD),
        sys_cache.reshape(SYS_DEV, 2 * HD),
        passage_place,
        passage_ids.T,
        passage_count,
        recompute_pos,
    )


def solution(mesh):
    placed = (
        P("req", "store"),
        P(),
        P(None, "store"),
        P(None, "store"),
        P(None, "store"),
        P("req", "store", None, None),
        P("req", "store", None),
        P(),
        P("req", None),
        P("req"),
        P("req", None),
    )
    return jax.shard_map(
        body, mesh=mesh, in_specs=placed, out_specs=P("req", "store"), check_vma=False
    )
```
